32 devices in a mesh: gx: 8 (over z, y), gy: 4 (over x, core).
Axes of the slice: x: 2, y: 2, z: 4, core: 2. Of those that a mesh axis runs over, the one named last changes fastest.
Arguments:
- disp: bfloat16 [2048, 4096], P(('gx', 'gy')), may hold values from -6 to 6
- adjoint: bfloat16 [2048, 4096], P(('gx', 'gy')), may hold values from -6 to 6
- tiles: bfloat16 [3072, 4096], P(('gx', 'gy')), may hold values from -0.75 to 0.75
- tile_rows: int32 [3072], P(('gx', 'gy')), may hold values from 0 to 63
- tile_cols: int32 [3072], P(('gx', 'gy')), may hold values from 0 to 95
- density: float32 [3072], P(('gx', 'gy')), may hold values from 0.1 to 1
- filter_weight: float32 [3072], P(('gx', 'gy')), may hold values from 0.2 to 2
- owner: int32 [3072, 1], P(('gx', 'gy')), may hold values from 0 to 3; in each aligned block of 96 rows (0 to 95, 96 to 191, ...) at most 96 rows name the same one
- region: int32 [3072], P(('gx', 'gy')), may hold values from 0 to 31
- face_x: int32 [32, 2, 12], P(('gx', 'gy')), may hold values from 0 to 63
- face_y: int32 [32, 2, 4], P(('gx', 'gy')), may hold values from 0 to 63
Outputs:
- filtered: float32 [1024, 128], P(('gx', 'gy'))
- compliance: float32 [64], replicated
The draws below stay inside these ranges and needn't reach their ends.
Inputs may be any that keep to these rules, and one draw needn't show every extreme that they name: Among the 96 elements of one subdomain at most 96 name the same owner, a bound that some block reaches.
All inputs are finite; a program needn't handle non-finite values.
Results may differ from the reference program's by a relative error of at most 0.0005.
Values may be sent and summed in bfloat16 or wider, within the bound.
A program may use at most 64 MiB of HBM per device.

```python
import math
import jax
import jax.numpy as jnp
import numpy as np
from jax import lax

BS = 64
R = 64
NB = 64
NT = 96
NIX = 12
NIY = 4
NREG = 32
CAP = 96
NGHOST = 96
BLOCKS = 2048
TILES = 3072
N_GX = 8
N_GY = 4
DEVICES = 32


def touch_ends(values, key, smallest, top_value):
    longest = values.shape.index(max(values.shape))
    spots = []
    for shift in (0, 1):
        where = [jax.random.randint(jax.random.fold_in(key, axis), (), 0, length) for axis, length in enumerate(values.shape)]
        where[longest] = (where[longest] + shift) % values.shape[longest]
        spots.append(tuple(where))
    return values.at[spots[0]].set(smallest).at[spots[1]].set(top_value)


def levels(stream_key, dims, pieces, least, largest):
    gain = 1.0
    for position, parts in pieces:
        steps = jax.random.uniform(jax.random.fold_in(jax.random.fold_in(stream_key, 6), position), (parts,), jnp.float32, least / len(pieces), largest / len(pieces))
        gain = gain * jnp.repeat(jnp.exp(steps), dims[position] // parts).reshape((-1,) + (1,) * (len(dims) - 1 - position))
    return gain


def deal_out(stream_key, own, number, rows, count, top, limit, lean):
    ranking = jax.random.permutation(stream_key, count)
    packed, ordinary = portions_of(count, rows * top, limit, lean, True), portions_of(count, rows * top, limit, lean, False)
    places = jnp.arange(count)

    def named(tallies, turn):
        used = int((tallies > 0).sum())
        fixed = max(1, used // 4)
        moved = fixed + (places - fixed + turn * (used - fixed)) % max(1, count - fixed)
        return jnp.zeros((count,), jnp.int32).at[ranking[jnp.where(places < fixed, places, moved)]].set(jnp.asarray(tallies, jnp.int32))

    tallies = jnp.where(number % 4 == 0, named(packed, number // 4), named(ordinary, number - number // 4 - 1))
    mixed = jax.random.permutation(jax.random.fold_in(own, 3), count)
    source_of, sink = mixed[0:count // 2 * 2:2], mixed[1:count // 2 * 2:2]
    margin = jnp.minimum(tallies[source_of] - 1, limit - tallies[sink]) // 2
    margin = jnp.where((source_of == ranking[0]) | (sink == ranking[0]) | (tallies[sink] == 0), 0, jnp.maximum(margin, 0))
    moved = jax.random.randint(jax.random.fold_in(own, 4), (count // 2,), 0, 1 << 20) % (margin + 1)
    tallies = tallies.at[source_of].add(-moved).at[sink].add(moved)
    labels = jnp.searchsorted(jnp.cumsum(tallies), jnp.arange(rows * top), side="right").astype(jnp.int32)
    table = labels.reshape(top, rows).T
    table = table[jax.random.permutation(jax.random.fold_in(own, 1), rows)]
    turn = jax.random.randint(jax.random.fold_in(own, 2), (rows, 1), 0, top)
    return jnp.take_along_axis(table, (jnp.arange(top)[None, :] + turn) % top, axis=1)


def portions_of(amount, total, most, slope, full):
    weights = [(1 << 20) // math.isqrt(grade ** slope) + 1 for grade in range(1, amount + 1)]
    largest = most if full else min(most, max(-(-total // amount), total * weights[0] // sum(weights)))
    least = 1 if total - largest >= amount - 1 else 0
    holding, surplus = [largest] + [least] * (amount - 1), total - largest - least * (amount - 1)
    while surplus > 0:
        free = [i for i in range(1, amount) if holding[i] < largest] or [i for i in range(1, amount) if holding[i] < most]
        whole, remaining = sum([weights[i] for i in free]), surplus
        for i in free:
            extra = min(most - holding[i], max(1, remaining * weights[i] // whole), surplus)
            holding[i] = holding[i] + extra
            surplus = surplus - extra
    return np.array(holding)


def centred(key, dims, spread, bound, pieces=(), kind=jnp.bfloat16):
    loudness = levels(key, dims, pieces, -0.22, 0.18) if pieces else 1.0
    values = jax.random.normal(key, dims, jnp.float32) * spread * loudness
    return jnp.minimum(jnp.maximum(values, -bound), bound).astype(kind)


def setup_inputs(seed: int = 0) -> dict:
    streams_of = jax.random.split(jax.random.key(seed), 12)
    disp = centred(streams_of[0], (BLOCKS, BS * R), 1.0, 6.0, ((0, 32),))
    adjoint = centred(streams_of[1], (BLOCKS, BS * R), 1.0, 6.0, ((0, 32),))
    tiles = centred(streams_of[2], (TILES, BS * BS), BS ** -0.5, 0.75, ((0, 32),))
    tile_rows = touch_ends(jax.random.randint(streams_of[3], (TILES,), 0, NB), jax.random.fold_in(streams_of[3], 1), 0, NB - 1).astype(jnp.int32)
    tile_cols = touch_ends(jax.random.randint(streams_of[4], (TILES,), 0, NGHOST), jax.random.fold_in(streams_of[4], 1), 0, NGHOST - 1).astype(jnp.int32)
    density = jnp.clip(0.1 + 0.9 * jax.random.uniform(streams_of[5], (TILES,), jnp.float32) ** levels(streams_of[5], (TILES,), ((0, 32),), -0.2, 0.2), 0.1, 1.0)
    filter_weight = jnp.clip(jnp.exp(math.log(2.0) - 2.3025851 * jax.random.uniform(streams_of[6], (TILES,), jnp.float32) ** levels(streams_of[6], (TILES,), ((0, 32),), -0.2, 0.2)), 0.2, 2.0)
    owner_keys = jax.random.split(jax.random.fold_in(streams_of[7], 1), TILES // NT)
    owner_turns = jax.random.permutation(jax.random.fold_in(streams_of[7], 3), TILES // NT)
    owner = jax.vmap(lambda own, number: deal_out(jax.random.fold_in(streams_of[7], 2), own, number, NT, N_GY, 1, CAP, 2))(owner_keys, owner_turns).reshape((TILES, 1))
    region = touch_ends(jax.random.randint(streams_of[8], (TILES,), 0, NREG), jax.random.fold_in(streams_of[8], 1), 0, NREG - 1).astype(jnp.int32)
    face_x = touch_ends(jax.random.randint(streams_of[9], (DEVICES, 2, NIX), 0, NB), jax.random.fold_in(streams_of[9], 1), 0, NB - 1).astype(jnp.int32)
    face_y = touch_ends(jax.random.randint(streams_of[10], (DEVICES, 2, NIY), 0, NB), jax.random.fold_in(streams_of[10], 1), 0, NB - 1).astype(jnp.int32)
    return dict(disp=disp, adjoint=adjoint, tiles=tiles, tile_rows=tile_rows, tile_cols=tile_cols, density=density, filter_weight=filter_weight, owner=owner, region=region, face_x=face_x, face_y=face_y)


def element_terms(args):
    uext, lext, tile, rows, cols, rho, weight = args
    kmat = tile.reshape(-1, BS, BS).astype(jnp.float32)
    ucol = uext[cols].reshape(-1, BS, R).astype(jnp.float32)
    lcol = lext[cols].reshape(-1, BS, R).astype(jnp.float32)
    ku = jnp.einsum('tjk,tkr->tjr', kmat, ucol)
    kl = jnp.einsum('tjk,tkr->tjr', kmat, lcol)
    urow = uext[rows].reshape(-1, BS, R).astype(jnp.float32)
    lrow = lext[rows].reshape(-1, BS, R).astype(jnp.float32)
    cross = lax.optimization_barrier(jnp.sum(lrow * ku + urow * kl, axis=1))
    energy = lax.optimization_barrier(jnp.sum(urow * ku, axis=1)) / math.sqrt(BS)
    sens = -(3.0 * rho * rho / (2.0 * math.sqrt(BS)))[:, None] * cross
    payload = weight[:, None] * jnp.concatenate([sens, energy], axis=1)
    return (payload, lax.optimization_barrier(jnp.sum(energy, axis=0)))

def extend(blocks, face_x, face_y):
    pick = jax.vmap(jax.vmap(lambda source, index: source[index]))
    sent_up_x = pick(blocks, face_x[:, :, 0])
    sent_down_x = pick(blocks, face_x[:, :, 1])
    sent_up_y = pick(blocks, face_y[:, :, 0])
    sent_down_y = pick(blocks, face_y[:, :, 1])
    low_x = jnp.concatenate([jnp.zeros_like(sent_up_x[:1]), sent_up_x[:-1]], axis=0)
    high_x = jnp.concatenate([sent_down_x[1:], jnp.zeros_like(sent_down_x[:1])], axis=0)
    low_y = jnp.concatenate([jnp.zeros_like(sent_up_y[:, :1]), sent_up_y[:, :-1]], axis=1)
    high_y = jnp.concatenate([sent_down_y[:, 1:], jnp.zeros_like(sent_down_y[:, :1])], axis=1)
    return jnp.concatenate([blocks, low_x, high_x, low_y, high_y], axis=2)

def reference(disp, adjoint, tiles, tile_rows, tile_cols, density, filter_weight, owner, region, face_x, face_y):
    count_x = N_GX
    count_y = N_GY
    ndev = count_x * count_y
    fx = face_x.reshape(count_x, count_y, 2, NIX)
    fy = face_y.reshape(count_x, count_y, 2, NIY)
    uext = extend(disp.reshape(count_x, count_y, NB, BS * R), fx, fy).reshape(ndev, NGHOST, BS * R)
    lext = extend(adjoint.reshape(count_x, count_y, NB, BS * R), fx, fy).reshape(ndev, NGHOST, BS * R)
    payload, energy = lax.map(element_terms, (uext, lext, tiles.reshape(ndev, NT, BS * BS), tile_rows.reshape(ndev, NT), tile_cols.reshape(ndev, NT), density.reshape(ndev, NT), filter_weight.reshape(ndev, NT)))
    column_base = jnp.arange(ndev, dtype=jnp.int32) // count_y * count_y
    owner_dev = column_base[:, None] + owner.reshape(ndev, NT)
    global_id = (owner_dev * NREG + region.reshape(ndev, NT)).reshape(-1)
    sums = jax.ops.segment_sum(payload.reshape(-1, 2 * R), global_id, ndev * NREG)
    totals = jax.ops.segment_sum(filter_weight, global_id, ndev * NREG)
    filtered = sums / jnp.maximum(totals, 1.0)[:, None]
    compliance = lax.optimization_barrier(jnp.sum(energy, axis=0)) / math.sqrt(ndev * NT)
    return (filtered, compliance)
```

```python
import functools
import math

import jax
import jax.numpy as jnp
from jax import lax
from jax.experimental import pallas as pl
from jax.experimental.pallas import tpu as pltpu
from jax.sharding import PartitionSpec as P

BS = 64
R = 64
NREG = 32
LANES = 2 * R
HALF = BS // 2
MESH = pl.DeviceIdType.MESH
BF16 = jnp.bfloat16
F32 = jnp.float32


def loop(count, unroll, body):
    def step(i, carry):
        for k in range(unroll):
            body(i * unroll + k)
        return carry

    lax.fori_loop(0, count // unroll, step, 0)


def exchange(src, dst, send_sem, recv_sem, where):
    return pltpu.make_async_remote_copy(
        src_ref=src,
        dst_ref=dst,
        send_sem=send_sem,
        recv_sem=recv_sem,
        device_id=where,
        device_id_type=MESH,
    )


def two_terms(x):
    high = x.astype(BF16)
    low = (x - high.astype(F32)).astype(BF16)
    return jnp.concatenate([high, low], axis=0)


def rows_by_region(onehot, x):
    doubled = jnp.concatenate([onehot, onehot], axis=0)
    return lax.dot_general(
        doubled, two_terms(x), (((0,), (0,)), ((), ())), preferred_element_type=F32
    )


def kernel(
    n_gx,
    n_gy,
    rows_ref,
    cols_ref,
    density_ref,
    weight_ref,
    owner_ref,
    region_ref,
    face_x_ref,
    face_y_ref,
    disp_hbm,
    adj_hbm,
    tiles_hbm,
    filtered_ref,
    compliance_ref,
    disp_raw,
    adj_raw,
    tiles_raw,
    disp_wide,
    adj_wide,
    tiles_wide,
    local,
    ext,
    staged,
    prod,
    prod_swapped,
    onehot,
    weights,
    partial,
    energy,
    totals_out,
    totals_in,
    sums_out,
    sums_in,
    comp_out,
    comp_in,
    load_sem,
    halo_send,
    halo_recv,
    totals_send,
    totals_recv,
    sums_send,
    sums_recv,
    comp_send,
    comp_recv,
):
    count = tiles_hbm.shape[0]
    blocks = disp_hbm.shape[0]
    nix = face_x_ref.shape[0] // 2
    niy = face_y_ref.shape[0] // 2
    gx = lax.axis_index("gx")
    gy = lax.axis_index("gy")

    loads = [
        pltpu.make_async_copy(src, dst, load_sem.at[k])
        for k, (src, dst) in enumerate(
            ((disp_hbm, disp_raw), (adj_hbm, adj_raw), (tiles_hbm, tiles_raw))
        )
    ]
    for load in loads:
        load.start()

    barrier = pltpu.get_barrier_semaphore()

    @pl.loop(0, n_gx)
    def _(i):
        @pl.when(i != gx)
        def _():
            pl.semaphore_signal(barrier, inc=1, device_id=(i, gy), device_id_type=MESH)

    @pl.loop(0, n_gy)
    def _(j):
        @pl.when(j != gy)
        def _():
            pl.semaphore_signal(barrier, inc=1, device_id=(gx, j), device_id_type=MESH)

    def widen(raw, wide, height):
        def body(c):
            chunk = raw[:, pl.ds(pl.multiple_of(c * LANES, LANES), LANES)]
            wide[pl.ds(pl.multiple_of(c * height, 8), height), :] = chunk.astype(F32)

        loop(HALF, 4, body)

    low_lanes = lax.broadcasted_iota(jnp.int32, (HALF, LANES), 1) < R

    loads[0].wait()
    widen(disp_raw, disp_wide, blocks)
    loads[1].wait()
    widen(adj_raw, adj_wide, blocks)

    def local_block(b):
        u = disp_wide[pl.ds(b, HALF, stride=blocks), :]
        a = adj_wide[pl.ds(b, HALF, stride=blocks), :]
        even = jnp.where(low_lanes, a, pltpu.roll(u, R, 1))
        odd = jnp.where(low_lanes, pltpu.roll(a, R, 1), u)
        block = jnp.concatenate([even, odd], axis=0).astype(BF16)
        local[b] = block
        ext[b] = block

    loop(blocks, 4, local_block)

    def stage(faces, first, number):
        def body(k):
            staged[first + k] = local[faces[k]]

        loop(number, 4, body)

    stage(face_x_ref, 0, 2 * nix)
    stage(face_y_ref, 2 * nix, 2 * niy)

    pl.semaphore_wait(barrier, n_gx + n_gy - 2)

    first = blocks
    plans = (
        (0, first, nix, gx < n_gx - 1, (gx + 1, gy), gx > 0),
        (nix, first + nix, nix, gx > 0, (gx - 1, gy), gx < n_gx - 1),
        (2 * nix, first + 2 * nix, niy, gy < n_gy - 1, (gx, gy + 1), gy > 0),
        (2 * nix + niy, first + 2 * nix + niy, niy, gy > 0, (gx, gy - 1), gy < n_gy - 1),
    )

    def halo(k):
        at, to, number, _, where, _ = plans[k]
        return exchange(
            staged.at[pl.ds(at, number)],
            ext.at[pl.ds(to, number)],
            halo_send.at[k],
            halo_recv.at[k],
            where,
        )

    for k, (_, to, number, has_target, _, has_source) in enumerate(plans):

        @pl.when(has_target)
        def _(k=k):
            halo(k).start()

        @pl.when(jnp.logical_not(has_source))
        def _(to=to, number=number):
            ext[pl.ds(to, number)] = jnp.zeros((number, BS, LANES), BF16)

    regions = n_gy * NREG
    key_lane = lax.broadcasted_iota(jnp.int32, (1, regions), 1)

    def key_row(t):
        key = owner_ref[t] * NREG + region_ref[t]
        onehot[pl.ds(t, 1), :] = (key_lane == key).astype(F32)
        weights[pl.ds(t, 1), :] = jnp.full((1, LANES), weight_ref[t], F32)

    loop(count, 4, key_row)
    hot = onehot[...].astype(BF16)
    totals_out[...] = rows_by_region(hot, weights[...]).reshape(n_gy, NREG, LANES)
    totals_in[gy] = totals_out[gy]

    def totals_copy(j, slot):
        return exchange(
            totals_out.at[j], totals_in.at[slot], totals_send.at[j], totals_recv.at[slot], (gx, j)
        )

    def sums_copy(j, slot):
        return exchange(
            sums_out.at[j], sums_in.at[slot], sums_send.at[j], sums_recv.at[slot], (gx, j)
        )

    def comp_copy(i, slot):
        return exchange(comp_out, comp_in.at[slot], comp_send.at[i], comp_recv.at[slot], (i, gy))

    def others(size, me, body):
        @pl.loop(0, size)
        def _(i):
            @pl.when(i != me)
            def _():
                body(i)

    others(n_gy, gy, lambda j: totals_copy(j, gy).start())

    loads[2].wait()
    widen(tiles_raw, tiles_wide, count)

    def product(t):
        pair = tiles_wide[pl.ds(t, HALF, stride=count), :]
        even = pair[:, :BS]
        odd = pltpu.roll(pair, BS, 1)[:, :BS]
        tile = jnp.concatenate([even, odd], axis=0).astype(BF16)
        block = local[rows_ref[t]]
        result = lax.dot_general(
            tile, block, (((0,), (0,)), ((), ())), preferred_element_type=F32
        )
        at = pl.ds(pl.multiple_of(t * BS, BS), BS)
        prod[at, :] = result
        prod_swapped[at, :] = pltpu.roll(result, R, 1)

    loop(count, 4, product)

    others(n_gy, gy, lambda j: totals_copy(j, j).wait_recv())
    total = jnp.zeros((NREG, LANES), F32)
    for j in range(n_gy):
        total = total + totals_in[j]
    scale = 1.0 / jnp.maximum(total, 1.0)

    for k, (_, _, _, _, _, has_source) in enumerate(plans):

        @pl.when(has_source)
        def _(k=k):
            halo(k).wait_recv()

    low8 = lax.broadcasted_iota(jnp.int32, (8, LANES), 1) < R

    def fold(x):
        parts = [x[8 * k : 8 * k + 8, :] for k in range(HALF // 8)]
        return (parts[0] + parts[1]) + (parts[2] + parts[3])

    def element(t):
        base = t * BS
        block = ext[cols_ref[t]]
        even = block[0:HALF, :].astype(F32)
        odd = block[HALF:BS, :].astype(F32)
        at_even = pl.ds(base, HALF, stride=2)
        at_odd = pl.ds(base + 1, HALF, stride=2)
        straight = fold(prod[at_even, :] * even + prod[at_odd, :] * odd)
        crossed = fold(prod_swapped[at_even, :] * even + prod_swapped[at_odd, :] * odd)
        cross = crossed + pltpu.roll(crossed, R, 1)
        strain = straight * (1.0 / math.sqrt(BS))
        rho = density_ref[t]
        sens = cross * (-(3.0 * rho * rho / (2.0 * math.sqrt(BS))))
        at = pl.ds(pl.multiple_of(t * 8, 8), 8)
        partial[at, :] = weight_ref[t] * jnp.where(low8, sens, strain)
        return strain

    unroll = 4

    def elements(i, total_energy):
        for k in range(unroll):
            total_energy = total_energy + element(i * unroll + k)
        return total_energy

    comp = lax.fori_loop(0, count // unroll, elements, jnp.zeros((8, LANES), F32))

    payload = partial[pl.ds(0, count, stride=8), :]
    for s in range(1, 8):
        payload = payload + partial[pl.ds(s, count, stride=8), :]
    sums_out[:, 0:NREG, :] = rows_by_region(hot, payload).reshape(n_gy, NREG, LANES)
    for j in range(n_gy):
        sums_out[j, NREG : NREG + 8, :] = comp
    sums_in[gy] = sums_out[gy]
    others(n_gy, gy, lambda j: sums_copy(j, gy).start())
    others(n_gy, gy, lambda j: sums_copy(j, j).wait_recv())
    gathered = sums_in[0]
    for j in range(1, n_gy):
        gathered = gathered + sums_in[j]
    comp_out[...] = gathered[NREG : NREG + 8, :]
    comp_in[gx] = comp_out[...]
    others(n_gx, gx, lambda i: comp_copy(i, gx).start())
    filtered_ref[...] = gathered[0:NREG, :] * scale

    for k, (_, _, _, has_target, _, _) in enumerate(plans):

        @pl.when(has_target)
        def _(k=k):
            halo(k).wait_send()

    others(n_gy, gy, lambda j: totals_copy(j, gy).wait_send())
    others(n_gy, gy, lambda j: sums_copy(j, gy).wait_send())

    others(n_gx, gx, lambda i: comp_copy(i, i).wait_recv())
    everything = lax.fori_loop(
        0, n_gx, lambda i, acc: acc + comp_in[i], jnp.zeros((8, LANES), F32)
    )
    line = jnp.sum(everything, axis=0, keepdims=True) / math.sqrt(count * n_gx * n_gy)
    compliance_ref[...] = pltpu.roll(jnp.broadcast_to(line, (8, LANES)), R, 1)[0:1, :]
    others(n_gx, gx, lambda i: comp_copy(i, gx).wait_send())


def shards(n_gx, n_gy, *args):
    (
        disp,
        adjoint,
        tiles,
        tile_rows,
        tile_cols,
        density,
        filter_weight,
        owner,
        region,
        face_x,
        face_y,
    ) = args
    count = tiles.shape[0]
    blocks = disp.shape[0]
    faces = face_x.shape[2] * 2 + face_y.shape[2] * 2
    smem = pl.BlockSpec(memory_space=pltpu.SMEM)
    hbm = pl.BlockSpec(memory_space=pl.ANY)
    vmem = pl.BlockSpec(memory_space=pltpu.VMEM)
    dma = pltpu.SemaphoreType.DMA
    filtered, compliance = pl.pallas_call(
        functools.partial(kernel, n_gx, n_gy),
        out_shape=(
            jax.ShapeDtypeStruct((NREG, LANES), F32),
            jax.ShapeDtypeStruct((1, LANES), F32),
        ),
        in_specs=[smem] * 8 + [hbm] * 3,
        out_specs=(vmem, vmem),
        scratch_shapes=[
            pltpu.VMEM((blocks, BS * R), BF16),
            pltpu.VMEM((blocks, BS * R), BF16),
            pltpu.VMEM((count, BS * BS), BF16),
            pltpu.VMEM((HALF * blocks, LANES), F32),
            pltpu.VMEM((HALF * blocks, LANES), F32),
            pltpu.VMEM((HALF * count, LANES), F32),
            pltpu.VMEM((blocks, BS, LANES), BF16),
            pltpu.VMEM((blocks + faces, BS, LANES), BF16),
            pltpu.VMEM((faces, BS, LANES), BF16),
            pltpu.VMEM((count * BS, LANES), F32),
            pltpu.VMEM((count * BS, LANES), F32),
            pltpu.VMEM((count, n_gy * NREG), F32),
            pltpu.VMEM((count, LANES), F32),
            pltpu.VMEM((count * 8, LANES), F32),
            pltpu.VMEM((8, LANES), F32),
            pltpu.VMEM((n_gy, NREG, LANES), F32),
            pltpu.VMEM((n_gy, NREG, LANES), F32),
            pltpu.VMEM((n_gy, NREG + 8, LANES), F32),
            pltpu.VMEM((n_gy, NREG + 8, LANES), F32),
            pltpu.VMEM((8, LANES), F32),
            pltpu.VMEM((n_gx, 8, LANES), F32),
            dma((3,)),
            dma((4,)),
            dma((4,)),
            dma((n_gy,)),
            dma((n_gy,)),
            dma((n_gy,)),
            dma((n_gy,)),
            dma((n_gx,)),
            dma((n_gx,)),
        ],
        compiler_params=pltpu.CompilerParams(
            collective_id=0, has_side_effects=True, vmem_limit_bytes=40 * 2**20
        ),
        name="sensitivities",
    )(
        tile_rows,
        tile_cols,
        density,
        filter_weight,
        owner.reshape(-1),
        region,
        face_x.reshape(-1),
        face_y.reshape(-1),
        disp,
        adjoint,
        tiles,
    )
    return filtered, compliance[0, :R]


def solution(mesh):
    placed = (
        P(("gx", "gy"), None),
        P(("gx", "gy"), None),
        P(("gx", "gy"), None),
        P(("gx", "gy")),
        P(("gx", "gy")),
        P(("gx", "gy")),
        P(("gx", "gy")),
        P(("gx", "gy"), None),
        P(("gx", "gy")),
        P(("gx", "gy"), None, None),
        P(("gx", "gy"), None, None),
    )
    return jax.shard_map(
        functools.partial(shards, mesh.shape["gx"], mesh.shape["gy"]),
        mesh=mesh,
        in_specs=placed,
        out_specs=(P(("gx", "gy"), None), P()),
        check_vma=False,
    )
```

```python
import functools
import math

import jax
import jax.numpy as jnp
from jax import lax
from jax.experimental import pallas as pl
from jax.experimental.pallas import tpu as pltpu
from jax.sharding import PartitionSpec as P

BS = 64
R = 64
NREG = 32
LANES = 2 * R
HALF = BS // 2
MESH = pl.DeviceIdType.MESH
BF16 = jnp.bfloat16
F32 = jnp.float32
I32 = jnp.int32


def loop(count, unroll, body):
    def step(i, carry):
        for k in range(unroll):
            body(i * unroll + k)
        return carry

    lax.fori_loop(0, count // unroll, step, 0)


def exchange(src, dst, send_sem, recv_sem, where):
    return pltpu.make_async_remote_copy(
        src_ref=src,
        dst_ref=dst,
        send_sem=send_sem,
        recv_sem=recv_sem,
        device_id=where,
        device_id_type=MESH,
    )


def two_terms(x):
    high = x.astype(BF16)
    low = (x - high.astype(F32)).astype(BF16)
    return jnp.concatenate([high, low], axis=0)


def rows_by_region(onehot, x):
    doubled = jnp.concatenate([onehot, onehot], axis=0)
    return lax.dot_general(
        doubled, two_terms(x), (((0,), (0,)), ((), ())), preferred_element_type=F32
    )


def kernel(
    n_gx,
    n_gy,
    rows_hbm,
    cols_hbm,
    density_hbm,
    weight_hbm,
    owner_hbm,
    region_hbm,
    face_x_hbm,
    face_y_hbm,
    disp_hbm,
    adj_hbm,
    tiles_hbm,
    filtered_ref,
    compliance_ref,
    rows_ref,
    cols_ref,
    density_ref,
    weight_ref,
    owner_ref,
    region_ref,
    face_x_ref,
    face_y_ref,
    disp_raw,
    adj_raw,
    tiles_raw,
    disp_wide,
    adj_wide,
    tiles_wide,
    local,
    ext,
    staged,
    prod,
    prod_swapped,
    onehot,
    weights,
    partial,
    energy,
    totals_out,
    totals_in,
    sums_out,
    sums_in,
    comp_out,
    comp_in,
    load_sem,
    halo_send,
    halo_recv,
    totals_send,
    totals_recv,
    sums_send,
    sums_recv,
    comp_send,
    comp_recv,
    scalar_sem,
    known_x,
    known_y,
):
    count = tiles_hbm.shape[0]
    blocks = disp_hbm.shape[0]
    nix = face_x_ref.shape[2]
    niy = face_y_ref.shape[2]
    gx = lax.axis_index("gx")
    gy = lax.axis_index("gy")

    barrier = pltpu.get_barrier_semaphore()

    def each_way(distance, body):
        for side, (place, size, where) in enumerate(
            ((gx, n_gx, lambda d: (gx + d, gy)), (gy, n_gy, lambda d: (gx, gy + d)))
        ):
            if distance < size:

                @pl.when(place + distance < size)
                def _(side=side, where=where):
                    body(side, 0, where(distance))

                @pl.when(place >= distance)
                def _(side=side, where=where):
                    body(side, 1, where(-distance))

    def greet(side, way, where):
        pl.semaphore_signal(barrier, inc=1, device_id=where, device_id_type=MESH)

    each_way(1, greet)

    loads = [
        pltpu.make_async_copy(src, dst, load_sem.at[k])
        for k, (src, dst) in enumerate(
            ((disp_hbm, disp_raw), (adj_hbm, adj_raw), (tiles_hbm, tiles_raw))
        )
    ]
    scalar_loads = [
        pltpu.make_async_copy(src, dst, scalar_sem.at[k])
        for k, (src, dst) in enumerate(
            (
                (face_x_hbm, face_x_ref),
                (face_y_hbm, face_y_ref),
                (rows_hbm, rows_ref),
                (cols_hbm, cols_ref),
                (density_hbm, density_ref),
                (weight_hbm, weight_ref),
                (owner_hbm, owner_ref),
                (region_hbm, region_ref),
            )
        )
    ]
    for load in loads[:2] + scalar_loads + loads[2:]:
        load.start()

    def learn_start(step):
        def body(side, way, where):
            known = known_x if side == 0 else known_y
            pl.semaphore_signal(
                known.at[step, way], inc=1, device_id=where, device_id_type=MESH
            )

        each_way(2**step, body)

    def learn_finish(step):
        def body(side, way, where):
            known = known_x if side == 0 else known_y
            pl.semaphore_wait(known.at[step, 1 - way], 1)

        each_way(2**step, body)

    steps = (max(n_gx, n_gy) - 1).bit_length()

    def widen(raw, wide, height):
        def body(c):
            chunk = raw[:, pl.ds(pl.multiple_of(c * LANES, LANES), LANES)]
            wide[pl.ds(pl.multiple_of(c * height, 8), height), :] = chunk.astype(F32)

        loop(HALF, 4, body)

    low_lanes = lax.broadcasted_iota(jnp.int32, (HALF, LANES), 1) < R

    loads[0].wait()
    widen(disp_raw, disp_wide, blocks)
    loads[1].wait()
    widen(adj_raw, adj_wide, blocks)

    def parts(b):
        u = disp_wide[pl.ds(b, HALF, stride=blocks), :]
        a = adj_wide[pl.ds(b, HALF, stride=blocks), :]
        u_turned = pltpu.roll(u, R, 1)
        a_turned = pltpu.roll(a, R, 1)
        even = jnp.where(low_lanes, a, u_turned)
        odd = jnp.where(low_lanes, a_turned, u)
        even_swapped = jnp.where(low_lanes, u, a_turned)
        odd_swapped = jnp.where(low_lanes, u_turned, a)
        block = jnp.concatenate([even, odd], axis=0).astype(BF16)
        swapped = jnp.concatenate([even_swapped, odd_swapped], axis=0).astype(BF16)
        return block, swapped

    def local_block(b):
        block, swapped = parts(b)
        local[b, :, 0:LANES] = block
        local[b, :, LANES : 2 * LANES] = swapped
        ext[b] = block

    def stage(faces, way, at, number):
        def body(k):
            staged[at + k] = parts(faces[0, way, k])[0]

        loop(number, 4, body)

    first = blocks
    plans = (
        (0, first, nix, gx < n_gx - 1, (gx + 1, gy), gx > 0),
        (nix, first + nix, nix, gx > 0, (gx - 1, gy), gx < n_gx - 1),
        (2 * nix, first + 2 * nix, niy, gy < n_gy - 1, (gx, gy + 1), gy > 0),
        (2 * nix + niy, first + 2 * nix + niy, niy, gy > 0, (gx, gy - 1), gy < n_gy - 1),
    )

    def halo(k):
        at, to, number, _, where, _ = plans[k]
        return exchange(
            staged.at[pl.ds(at, number)],
            ext.at[pl.ds(to, number)],
            halo_send.at[k],
            halo_recv.at[k],
            where,
        )

    for load in scalar_loads[:2]:
        load.wait()
    for k, (at, to, number, has_target, _, has_source) in enumerate(plans):
        stage(face_x_ref if k < 2 else face_y_ref, k % 2, at, number)
        if k == 0:
            neighbours = (
                (gx > 0).astype(jnp.int32)
                + (gx < n_gx - 1).astype(jnp.int32)
                + (gy > 0).astype(jnp.int32)
                + (gy < n_gy - 1).astype(jnp.int32)
            )
            pl.semaphore_wait(barrier, neighbours)

        @pl.when(has_target)
        def _(k=k):
            halo(k).start()

        @pl.when(jnp.logical_not(has_source))
        def _(to=to, number=number):
            ext[pl.ds(to, number)] = jnp.zeros((number, BS, LANES), BF16)

    learn_start(0)
    loop(blocks, 4, local_block)
    learn_finish(0)
    for step in range(1, steps):
        learn_start(step)
        if step < steps - 1:
            learn_finish(step)
    for load in scalar_loads[2:]:
        load.wait()

    regions = n_gy * NREG
    key_lane = lax.broadcasted_iota(jnp.int32, (1, regions), 1)

    def key_row(t):
        key = owner_ref[t] * NREG + region_ref[t]
        onehot[pl.ds(t, 1), :] = (key_lane == key).astype(F32)
        weights[pl.ds(t, 1), :] = jnp.full((1, LANES), weight_ref[t], F32)

    loop(count, 4, key_row)
    hot = onehot[...].astype(BF16)
    totals_out[...] = rows_by_region(hot, weights[...]).reshape(n_gy, NREG, LANES)
    totals_in[gy] = totals_out[gy]

    def totals_copy(j, slot):
        return exchange(
            totals_out.at[j], totals_in.at[slot], totals_send.at[j], totals_recv.at[slot], (gx, j)
        )

    def sums_copy(j, slot):
        return exchange(
            sums_out.at[j], sums_in.at[slot], sums_send.at[j], sums_recv.at[slot], (gx, j)
        )

    def comp_copy(i, slot):
        return exchange(comp_out, comp_in.at[slot], comp_send.at[i], comp_recv.at[slot], (i, gy))

    def others(size, me, body):
        @pl.loop(0, size)
        def _(i):
            @pl.when(i != me)
            def _():
                body(i)

    loads[2].wait()
    widen(tiles_raw, tiles_wide, count)

    def products(i):
        t = 2 * i
        one = tiles_wide[pl.ds(t, HALF, stride=count), :]
        two = tiles_wide[pl.ds(t + 1, HALF, stride=count), :]
        even = jnp.where(low_lanes, one, pltpu.roll(two, BS, 1))
        odd = jnp.where(low_lanes, pltpu.roll(one, BS, 1), two)
        turned = jnp.concatenate([even, odd], axis=0).astype(BF16).T
        for k in range(2):
            result = jnp.dot(
                turned[k * BS : (k + 1) * BS, :],
                local[rows_ref[t + k]],
                preferred_element_type=F32,
            )
            at = pl.ds(pl.multiple_of((t + k) * BS, BS), BS)
            prod[at, :] = result[:, 0:LANES]
            prod_swapped[at, :] = result[:, LANES : 2 * LANES]

    loop(count // 2, 2, products)
    if steps > 1:
        learn_finish(steps - 1)
    others(n_gy, gy, lambda j: totals_copy(j, gy).start())

    others(n_gy, gy, lambda j: totals_copy(j, j).wait_recv())
    total = jnp.zeros((NREG, LANES), F32)
    for j in range(n_gy):
        total = total + totals_in[j]
    scale = 1.0 / jnp.maximum(total, 1.0)

    for k, (_, _, _, _, _, has_source) in enumerate(plans):

        @pl.when(has_source)
        def _(k=k):
            halo(k).wait_recv()

    low8 = lax.broadcasted_iota(jnp.int32, (8, LANES), 1) < R

    def fold(x):
        parts = [x[8 * k : 8 * k + 8, :] for k in range(HALF // 8)]
        return (parts[0] + parts[1]) + (parts[2] + parts[3])

    def element(t):
        base = t * BS
        block = ext[cols_ref[t]]
        even = block[0:HALF, :].astype(F32)
        odd = block[HALF:BS, :].astype(F32)
        at_even = pl.ds(base, HALF, stride=2)
        at_odd = pl.ds(base + 1, HALF, stride=2)
        straight = fold(prod[at_even, :] * even + prod[at_odd, :] * odd)
        crossed = fold(prod_swapped[at_even, :] * even + prod_swapped[at_odd, :] * odd)
        cross = crossed + pltpu.roll(crossed, R, 1)
        strain = straight * (1.0 / math.sqrt(BS))
        rho = density_ref[t]
        sens = cross * (-(3.0 * rho * rho / (2.0 * math.sqrt(BS))))
        at = pl.ds(pl.multiple_of(t * 8, 8), 8)
        partial[at, :] = weight_ref[t] * jnp.where(low8, sens, strain)
        return strain

    unroll = 4

    def elements(i, total_energy):
        for k in range(unroll):
            total_energy = total_energy + element(i * unroll + k)
        return total_energy

    comp = lax.fori_loop(0, count // unroll, elements, jnp.zeros((8, LANES), F32))

    payload = partial[pl.ds(0, count, stride=8), :]
    for s in range(1, 8):
        payload = payload + partial[pl.ds(s, count, stride=8), :]
    sums_out[:, 0:NREG, :] = rows_by_region(hot, payload).reshape(n_gy, NREG, LANES)
    for j in range(n_gy):
        sums_out[j, NREG : NREG + 8, :] = comp
    sums_in[gy] = sums_out[gy]
    others(n_gy, gy, lambda j: sums_copy(j, gy).start())
    others(n_gy, gy, lambda j: sums_copy(j, j).wait_recv())
    gathered = sums_in[0]
    for j in range(1, n_gy):
        gathered = gathered + sums_in[j]
    comp_out[...] = gathered[NREG : NREG + 8, :]
    comp_in[gx] = comp_out[...]
    others(n_gx, gx, lambda i: comp_copy(i, gx).start())
    filtered_ref[...] = gathered[0:NREG, :] * scale

    for k, (_, _, _, has_target, _, _) in enumerate(plans):

        @pl.when(has_target)
        def _(k=k):
            halo(k).wait_send()

    others(n_gy, gy, lambda j: totals_copy(j, gy).wait_send())
    others(n_gy, gy, lambda j: sums_copy(j, gy).wait_send())

    others(n_gx, gx, lambda i: comp_copy(i, i).wait_recv())
    everything = lax.fori_loop(
        0, n_gx, lambda i, acc: acc + comp_in[i], jnp.zeros((8, LANES), F32)
    )
    line = jnp.sum(everything, axis=0, keepdims=True) / math.sqrt(count * n_gx * n_gy)
    compliance_ref[...] = pltpu.roll(jnp.broadcast_to(line, (8, LANES)), R, 1)[0:1, :]
    others(n_gx, gx, lambda i: comp_copy(i, gx).wait_send())


def shards(n_gx, n_gy, *args):
    (
        disp,
        adjoint,
        tiles,
        tile_rows,
        tile_cols,
        density,
        filter_weight,
        owner,
        region,
        face_x,
        face_y,
    ) = args
    count = tiles.shape[0]
    blocks = disp.shape[0]
    faces = face_x.shape[2] * 2 + face_y.shape[2] * 2
    hbm = pl.BlockSpec(memory_space=pltpu.HBM)
    steps = (max(n_gx, n_gy) - 1).bit_length()
    vmem = pl.BlockSpec(memory_space=pltpu.VMEM)
    dma = pltpu.SemaphoreType.DMA
    filtered, compliance = pl.pallas_call(
        functools.partial(kernel, n_gx, n_gy),
        out_shape=(
            jax.ShapeDtypeStruct((NREG, LANES), F32),
            jax.ShapeDtypeStruct((1, LANES), F32),
        ),
        in_specs=[hbm] * 11,
        out_specs=(vmem, vmem),
        scratch_shapes=[
            *(pltpu.SMEM((count,), kind) for kind in (I32, I32, F32, F32, I32, I32)),
            pltpu.SMEM(face_x.shape, I32),
            pltpu.SMEM(face_y.shape, I32),
            pltpu.VMEM((blocks, BS * R), BF16),
            pltpu.VMEM((blocks, BS * R), BF16),
            pltpu.VMEM((count, BS * BS), BF16),
            pltpu.VMEM((HALF * blocks, LANES), F32),
            pltpu.VMEM((HALF * blocks, LANES), F32),
            pltpu.VMEM((HALF * count, LANES), F32),
            pltpu.VMEM((blocks, BS, 2 * LANES), BF16),
            pltpu.VMEM((blocks + faces, BS, LANES), BF16),
            pltpu.VMEM((faces, BS, LANES), BF16),
            pltpu.VMEM((count * BS, LANES), F32),
            pltpu.VMEM((count * BS, LANES), F32),
            pltpu.VMEM((count, n_gy * NREG), F32),
            pltpu.VMEM((count, LANES), F32),
            pltpu.VMEM((count * 8, LANES), F32),
            pltpu.VMEM((8, LANES), F32),
            pltpu.VMEM((n_gy, NREG, LANES), F32),
            pltpu.VMEM((n_gy, NREG, LANES), F32),
            pltpu.VMEM((n_gy, NREG + 8, LANES), F32),
            pltpu.VMEM((n_gy, NREG + 8, LANES), F32),
            pltpu.VMEM((8, LANES), F32),
            pltpu.VMEM((n_gx, 8, LANES), F32),
            dma((3,)),
            dma((4,)),
            dma((4,)),
            dma((n_gy,)),
            dma((n_gy,)),
            dma((n_gy,)),
            dma((n_gy,)),
            dma((n_gx,)),
            dma((n_gx,)),
            dma((8,)),
            pltpu.SemaphoreType.REGULAR((steps, 2)),
            pltpu.SemaphoreType.REGULAR((steps, 2)),
        ],
        compiler_params=pltpu.CompilerParams(
            collective_id=0, has_side_effects=True, vmem_limit_bytes=60 * 2**20
        ),
        name="sensitivities",
    )(
        tile_rows,
        tile_cols,
        density,
        filter_weight,
        owner.reshape(-1),
        region,
        face_x,
        face_y,
        disp,
        adjoint,
        tiles,
    )
    return filtered, compliance[0, :R]


def solution(mesh):
    placed = (
        P(("gx", "gy"), None),
        P(("gx", "gy"), None),
        P(("gx", "gy"), None),
        P(("gx", "gy")),
        P(("gx", "gy")),
        P(("gx", "gy")),
        P(("gx", "gy")),
        P(("gx", "gy"), None),
        P(("gx", "gy")),
        P(("gx", "gy"), None, None),
        P(("gx", "gy"), None, None),
    )
    return jax.shard_map(
        functools.partial(shards, mesh.shape["gx"], mesh.shape["gy"]),
        mesh=mesh,
        in_specs=placed,
        out_specs=(P(("gx", "gy"), None), P()),
        check_vma=False,
    )
```

```python
import functools
import math

import jax
import jax.numpy as jnp
from jax import lax
from jax.experimental import pallas as pl
from jax.experimental.pallas import tpu as pltpu
from jax.sharding import PartitionSpec as P

BS = 64
R = 64
NREG = 32
LANES = 2 * R
HALF = BS // 2
MESH = pl.DeviceIdType.MESH
BF16 = jnp.bfloat16
F32 = jnp.float32
I32 = jnp.int32


def loop(count, unroll, body):
    def step(i, carry):
        for k in range(unroll):
            body(i * unroll + k)
        return carry

    lax.fori_loop(0, count // unroll, step, 0)


def exchange(src, dst, send_sem, recv_sem, where):
    return pltpu.make_async_remote_copy(
        src_ref=src,
        dst_ref=dst,
        send_sem=send_sem,
        recv_sem=recv_sem,
        device_id=where,
        device_id_type=MESH,
    )


def two_terms(x):
    high = x.astype(BF16)
    low = (x - high.astype(F32)).astype(BF16)
    return jnp.concatenate([high, low], axis=0)


def rows_by_region(onehot, x):
    doubled = jnp.concatenate([onehot, onehot], axis=0)
    return lax.dot_general(
        doubled, two_terms(x), (((0,), (0,)), ((), ())), preferred_element_type=F32
    )


def kernel(
    n_gx,
    n_gy,
    rows_hbm,
    cols_hbm,
    density_hbm,
    weight_hbm,
    owner_hbm,
    region_hbm,
    face_x_hbm,
    face_y_hbm,
    disp_hbm,
    adj_hbm,
    tiles_hbm,
    filtered_ref,
    compliance_ref,
    rows_ref,
    cols_ref,
    density_ref,
    weight_ref,
    owner_ref,
    region_ref,
    face_x_ref,
    face_y_ref,
    disp_raw,
    adj_raw,
    tiles_raw,
    disp_wide,
    adj_wide,
    tiles_wide,
    local,
    ext,
    staged,
    prod,
    prod_swapped,
    onehot,
    weights,
    partial,
    energy,
    totals_out,
    totals_in,
    sums_out,
    sums_in,
    comp_out,
    comp_in,
    load_sem,
    halo_send,
    halo_recv,
    totals_send,
    totals_recv,
    sums_send,
    sums_recv,
    comp_send,
    comp_recv,
    scalar_sem,
    known_x,
    known_y,
):
    count = tiles_hbm.shape[0]
    blocks = disp_hbm.shape[0]
    nix = face_x_ref.shape[2]
    niy = face_y_ref.shape[2]
    gx = lax.axis_index("gx")
    gy = lax.axis_index("gy")

    barrier = pltpu.get_barrier_semaphore()

    def each_way(distance, body):
        for side, (place, size, where) in enumerate(
            ((gx, n_gx, lambda d: (gx + d, gy)), (gy, n_gy, lambda d: (gx, gy + d)))
        ):
            if distance < size:

                @pl.when(place + distance < size)
                def _(side=side, where=where):
                    body(side, 0, where(distance))

                @pl.when(place >= distance)
                def _(side=side, where=where):
                    body(side, 1, where(-distance))

    def greet(side, way, where):
        pl.semaphore_signal(barrier, inc=1, device_id=where, device_id_type=MESH)

    each_way(1, greet)

    loads = [
        pltpu.make_async_copy(src, dst, load_sem.at[k])
        for k, (src, dst) in enumerate(
            ((disp_hbm, disp_raw), (adj_hbm, adj_raw), (tiles_hbm, tiles_raw))
        )
    ]
    scalar_loads = [
        pltpu.make_async_copy(src, dst, scalar_sem.at[k])
        for k, (src, dst) in enumerate(
            (
                (face_x_hbm, face_x_ref),
                (face_y_hbm, face_y_ref),
                (rows_hbm, rows_ref),
                (cols_hbm, cols_ref),
                (density_hbm, density_ref),
                (weight_hbm, weight_ref),
                (owner_hbm, owner_ref),
                (region_hbm, region_ref),
            )
        )
    ]
    for load in loads[:2] + scalar_loads + loads[2:]:
        load.start()

    def learn_start(step):
        def body(side, way, where):
            known = known_x if side == 0 else known_y
            pl.semaphore_signal(
                known.at[step, way], inc=1, device_id=where, device_id_type=MESH
            )

        each_way(2**step, body)

    def learn_finish(step):
        def body(side, way, where):
            known = known_x if side == 0 else known_y
            pl.semaphore_wait(known.at[step, 1 - way], 1)

        each_way(2**step, body)

    steps = (max(n_gx, n_gy) - 1).bit_length()

    def widen(raw, wide, height):
        def body(c):
            chunk = raw[:, pl.ds(pl.multiple_of(c * LANES, LANES), LANES)]
            wide[pl.ds(c * (height + 1), height), :] = chunk.astype(F32)

        loop(HALF, 4, body)

    low_lanes = lax.broadcasted_iota(jnp.int32, (HALF, LANES), 1) < R

    loads[0].wait()
    widen(disp_raw, disp_wide, blocks)
    loads[1].wait()
    widen(adj_raw, adj_wide, blocks)

    def parts(b):
        u = disp_wide[pl.ds(b, HALF, stride=blocks + 1), :]
        a = adj_wide[pl.ds(b, HALF, stride=blocks + 1), :]
        u_turned = pltpu.roll(u, R, 1)
        a_turned = pltpu.roll(a, R, 1)
        even = jnp.where(low_lanes, a, u_turned)
        odd = jnp.where(low_lanes, a_turned, u)
        even_swapped = jnp.where(low_lanes, u, a_turned)
        odd_swapped = jnp.where(low_lanes, u_turned, a)
        block = jnp.concatenate([even, odd], axis=0).astype(BF16)
        swapped = jnp.concatenate([even_swapped, odd_swapped], axis=0).astype(BF16)
        return block, swapped

    def local_block(b):
        block, swapped = parts(b)
        local[b, :, 0:LANES] = block
        local[b, :, LANES : 2 * LANES] = swapped
        ext[b] = block

    def stage(faces, way, at, number):
        def body(k):
            staged[at + k] = parts(faces[0, way, k])[0]

        loop(number, 4, body)

    first = blocks
    plans = (
        (0, first, nix, gx < n_gx - 1, (gx + 1, gy), gx > 0),
        (nix, first + nix, nix, gx > 0, (gx - 1, gy), gx < n_gx - 1),
        (2 * nix, first + 2 * nix, niy, gy < n_gy - 1, (gx, gy + 1), gy > 0),
        (2 * nix + niy, first + 2 * nix + niy, niy, gy > 0, (gx, gy - 1), gy < n_gy - 1),
    )

    def halo(k):
        at, to, number, _, where, _ = plans[k]
        return exchange(
            staged.at[pl.ds(at, number)],
            ext.at[pl.ds(to, number)],
            halo_send.at[k],
            halo_recv.at[k],
            where,
        )

    for load in scalar_loads[:2]:
        load.wait()
    for k, (at, to, number, has_target, _, has_source) in enumerate(plans):
        stage(face_x_ref if k < 2 else face_y_ref, k % 2, at, number)
        if k == 0:
            neighbours = (
                (gx > 0).astype(jnp.int32)
                + (gx < n_gx - 1).astype(jnp.int32)
                + (gy > 0).astype(jnp.int32)
                + (gy < n_gy - 1).astype(jnp.int32)
            )
            pl.semaphore_wait(barrier, neighbours)

        @pl.when(has_target)
        def _(k=k):
            halo(k).start()

        @pl.when(jnp.logical_not(has_source))
        def _(to=to, number=number):
            ext[pl.ds(to, number)] = jnp.zeros((number, BS, LANES), BF16)

    learn_start(0)
    loop(blocks, 4, local_block)
    learn_finish(0)
    for step in range(1, steps):
        learn_start(step)
        if step < steps - 1:
            learn_finish(step)
    for load in scalar_loads[2:]:
        load.wait()

    regions = n_gy * NREG
    key_lane = lax.broadcasted_iota(jnp.int32, (1, regions), 1)

    def key_row(t):
        key = owner_ref[t] * NREG + region_ref[t]
        onehot[pl.ds(t, 1), :] = (key_lane == key).astype(F32)
        weights[pl.ds(t, 1), :] = jnp.full((1, LANES), weight_ref[t], F32)

    loop(count, 4, key_row)
    hot = onehot[...].astype(BF16)
    totals_out[...] = rows_by_region(hot, weights[...]).reshape(n_gy, NREG, LANES)
    totals_in[gy] = totals_out[gy]

    def totals_copy(j, slot):
        return exchange(
            totals_out.at[j], totals_in.at[slot], totals_send.at[j], totals_recv.at[slot], (gx, j)
        )

    def sums_copy(j, slot):
        return exchange(
            sums_out.at[j], sums_in.at[slot], sums_send.at[j], sums_recv.at[slot], (gx, j)
        )

    def comp_copy(i, slot):
        return exchange(comp_out, comp_in.at[slot], comp_send.at[i], comp_recv.at[slot], (i, gy))

    def others(size, me, body):
        @pl.loop(0, size)
        def _(i):
            @pl.when(i != me)
            def _():
                body(i)

    loads[2].wait()
    widen(tiles_raw, tiles_wide, count)

    def products(i):
        t = 2 * i
        one = tiles_wide[pl.ds(t, HALF, stride=count + 1), :]
        two = tiles_wide[pl.ds(t + 1, HALF, stride=count + 1), :]
        even = jnp.where(low_lanes, one, pltpu.roll(two, BS, 1))
        odd = jnp.where(low_lanes, pltpu.roll(one, BS, 1), two)
        turned = jnp.concatenate([even, odd], axis=0).astype(BF16).T
        for k in range(2):
            result = jnp.dot(
                turned[k * BS : (k + 1) * BS, :],
                local[rows_ref[t + k]],
                preferred_element_type=F32,
            )
            at = pl.ds(pl.multiple_of((t + k) * BS, BS), BS)
            prod[at, :] = result[:, 0:LANES]
            prod_swapped[at, :] = result[:, LANES : 2 * LANES]

    loop(count // 2, 2, products)
    if steps > 1:
        learn_finish(steps - 1)
    others(n_gy, gy, lambda j: totals_copy(j, gy).start())

    for k, (_, _, _, _, _, has_source) in enumerate(plans):

        @pl.when(has_source)
        def _(k=k):
            halo(k).wait_recv()

    low8 = lax.broadcasted_iota(jnp.int32, (8, LANES), 1) < R

    def fold(x):
        parts = [x[8 * k : 8 * k + 8, :] for k in range(HALF // 8)]
        return (parts[0] + parts[1]) + (parts[2] + parts[3])

    def element(t):
        base = t * BS
        block = ext[cols_ref[t]]
        even = block[0:HALF, :].astype(F32)
        odd = block[HALF:BS, :].astype(F32)
        at_even = pl.ds(base, HALF, stride=2)
        at_odd = pl.ds(base + 1, HALF, stride=2)
        straight = fold(prod[at_even, :] * even + prod[at_odd, :] * odd)
        crossed = fold(prod_swapped[at_even, :] * even + prod_swapped[at_odd, :] * odd)
        cross = crossed + pltpu.roll(crossed, R, 1)
        strain = straight * (1.0 / math.sqrt(BS))
        rho = density_ref[t]
        sens = cross * (-(3.0 * rho * rho / (2.0 * math.sqrt(BS))))
        at = pl.ds(t * 9, 8)
        partial[at, :] = weight_ref[t] * jnp.where(low8, sens, strain)
        return strain

    unroll = 4

    def elements(i, total_energy):
        for k in range(unroll):
            total_energy = total_energy + element(i * unroll + k)
        return total_energy

    comp = lax.fori_loop(0, count // unroll, elements, jnp.zeros((8, LANES), F32))

    payload = partial[pl.ds(0, count, stride=9), :]
    for s in range(1, 8):
        payload = payload + partial[pl.ds(s, count, stride=9), :]
    sums_out[:, 0:NREG, :] = rows_by_region(hot, payload).reshape(n_gy, NREG, LANES)
    for j in range(n_gy):
        sums_out[j, NREG : NREG + 8, :] = comp
    sums_in[gy] = sums_out[gy]
    others(n_gy, gy, lambda j: sums_copy(j, gy).start())
    others(n_gy, gy, lambda j: sums_copy(j, j).wait_recv())
    gathered = sums_in[0]
    for j in range(1, n_gy):
        gathered = gathered + sums_in[j]
    comp_out[...] = gathered[NREG : NREG + 8, :]
    comp_in[gx] = comp_out[...]
    others(n_gx, gx, lambda i: comp_copy(i, gx).start())
    others(n_gy, gy, lambda j: totals_copy(j, j).wait_recv())
    total = jnp.zeros((NREG, LANES), F32)
    for j in range(n_gy):
        total = total + totals_in[j]
    scale = 1.0 / jnp.maximum(total, 1.0)
    filtered_ref[...] = gathered[0:NREG, :] * scale

    for k, (_, _, _, has_target, _, _) in enumerate(plans):

        @pl.when(has_target)
        def _(k=k):
            halo(k).wait_send()

    others(n_gy, gy, lambda j: totals_copy(j, gy).wait_send())
    others(n_gy, gy, lambda j: sums_copy(j, gy).wait_send())

    others(n_gx, gx, lambda i: comp_copy(i, i).wait_recv())
    everything = lax.fori_loop(
        0, n_gx, lambda i, acc: acc + comp_in[i], jnp.zeros((8, LANES), F32)
    )
    line = jnp.sum(everything, axis=0, keepdims=True) / math.sqrt(count * n_gx * n_gy)
    turned_line = pltpu.roll(jnp.broadcast_to(line, (8, LANES)), R, 1)
    compliance_ref[...] = turned_line[0, 0:R]
    others(n_gx, gx, lambda i: comp_copy(i, gx).wait_send())


def shards(n_gx, n_gy, *args):
    (
        disp,
        adjoint,
        tiles,
        tile_rows,
        tile_cols,
        density,
        filter_weight,
        owner,
        region,
        face_x,
        face_y,
    ) = args
    count = tiles.shape[0]
    blocks = disp.shape[0]
    faces = face_x.shape[2] * 2 + face_y.shape[2] * 2
    hbm = pl.BlockSpec(memory_space=pltpu.HBM)
    steps = (max(n_gx, n_gy) - 1).bit_length()
    vmem = pl.BlockSpec(memory_space=pltpu.VMEM)
    dma = pltpu.SemaphoreType.DMA
    filtered, compliance = pl.pallas_call(
        functools.partial(kernel, n_gx, n_gy),
        out_shape=(
            jax.ShapeDtypeStruct((NREG, LANES), F32),
            jax.ShapeDtypeStruct((R,), F32),
        ),
        in_specs=[hbm] * 11,
        out_specs=(vmem, vmem),
        scratch_shapes=[
            *(pltpu.SMEM((count,), kind) for kind in (I32, I32, F32, F32, I32, I32)),
            pltpu.SMEM(face_x.shape, I32),
            pltpu.SMEM(face_y.shape, I32),
            pltpu.VMEM((blocks, BS * R), BF16),
            pltpu.VMEM((blocks, BS * R), BF16),
            pltpu.VMEM((count, BS * BS), BF16),
            pltpu.VMEM((HALF * (blocks + 1), LANES), F32),
            pltpu.VMEM((HALF * (blocks + 1), LANES), F32),
            pltpu.VMEM((HALF * (count + 1), LANES), F32),
            pltpu.VMEM((blocks, BS, 2 * LANES), BF16),
            pltpu.VMEM((blocks + faces, BS, LANES), BF16),
            pltpu.VMEM((faces, BS, LANES), BF16),
            pltpu.VMEM((count * BS, LANES), F32),
            pltpu.VMEM((count * BS, LANES), F32),
            pltpu.VMEM((count, n_gy * NREG), F32),
            pltpu.VMEM((count, LANES), F32),
            pltpu.VMEM((count * 9, LANES), F32),
            pltpu.VMEM((8, LANES), F32),
            pltpu.VMEM((n_gy, NREG, LANES), F32),
            pltpu.VMEM((n_gy, NREG, LANES), F32),
            pltpu.VMEM((n_gy, NREG + 8, LANES), F32),
            pltpu.VMEM((n_gy, NREG + 8, LANES), F32),
            pltpu.VMEM((8, LANES), F32),
            pltpu.VMEM((n_gx, 8, LANES), F32),
            dma((3,)),
            dma((4,)),
            dma((4,)),
            dma((n_gy,)),
            dma((n_gy,)),
            dma((n_gy,)),
            dma((n_gy,)),
            dma((n_gx,)),
            dma((n_gx,)),
            dma((8,)),
            pltpu.SemaphoreType.REGULAR((steps, 2)),
            pltpu.SemaphoreType.REGULAR((steps, 2)),
        ],
        compiler_params=pltpu.CompilerParams(
            collective_id=0, has_side_effects=True, vmem_limit_bytes=60 * 2**20
        ),
        name="sensitivities",
    )(
        tile_rows,
        tile_cols,
        density,
        filter_weight,
        owner.reshape(-1),
        region,
        face_x,
        face_y,
        disp,
        adjoint,
        tiles,
    )
    return filtered, compliance


def solution(mesh):
    placed = (
        P(("gx", "gy"), None),
        P(("gx", "gy"), None),
        P(("gx", "gy"), None),
        P(("gx", "gy")),
        P(("gx", "gy")),
        P(("gx", "gy")),
        P(("gx", "gy")),
        P(("gx", "gy"), None),
        P(("gx", "gy")),
        P(("gx", "gy"), None, None),
        P(("gx", "gy"), None, None),
    )
    return jax.shard_map(
        functools.partial(shards, mesh.shape["gx"], mesh.shape["gy"]),
        mesh=mesh,
        in_specs=placed,
        out_specs=(P(("gx", "gy"), None), P()),
        check_vma=False,
    )
```

```python
import functools
import math

import jax
import jax.numpy as jnp
from jax import lax
from jax.experimental import pallas as pl
from jax.experimental.pallas import tpu as pltpu
from jax.sharding import PartitionSpec as P

BS = 64
R = 64
NREG = 32
LANES = 2 * R
HALF = BS // 2
MESH = pl.DeviceIdType.MESH
BF16 = jnp.bfloat16
F32 = jnp.float32
I32 = jnp.int32


def loop(count, unroll, read, write):
    def step(i, carry):
        places = [i * unroll + k for k in range(unroll)]
        values = [read(place) for place in places]
        for place, value in zip(places, values):
            write(place, value)
        return carry

    lax.fori_loop(0, count // unroll, step, 0)


def exchange(src, dst, send_sem, recv_sem, where):
    return pltpu.make_async_remote_copy(
        src_ref=src,
        dst_ref=dst,
        send_sem=send_sem,
        recv_sem=recv_sem,
        device_id=where,
        device_id_type=MESH,
    )


def two_terms(x):
    high = x.astype(BF16)
    low = (x - high.astype(F32)).astype(BF16)
    return jnp.concatenate([high, low], axis=0)


def rows_by_region(onehot, x):
    doubled = jnp.concatenate([onehot, onehot], axis=0)
    return lax.dot_general(
        doubled, two_terms(x), (((0,), (0,)), ((), ())), preferred_element_type=F32
    )


def kernel(
    n_gx,
    n_gy,
    rows_hbm,
    cols_hbm,
    density_hbm,
    weight_hbm,
    owner_hbm,
    region_hbm,
    face_x_hbm,
    face_y_hbm,
    disp_hbm,
    adj_hbm,
    tiles_hbm,
    filtered_ref,
    compliance_ref,
    rows_ref,
    cols_ref,
    density_ref,
    weight_ref,
    owner_ref,
    region_ref,
    face_x_ref,
    face_y_ref,
    disp_raw,
    adj_raw,
    tiles_raw,
    disp_wide,
    adj_wide,
    tiles_wide,
    turned,
    local,
    ext,
    staged,
    prod,
    prod_swapped,
    onehot,
    weights,
    partial,
    energy,
    totals_out,
    totals_in,
    sums_out,
    sums_in,
    comp_out,
    comp_in,
    load_sem,
    halo_send,
    halo_recv,
    totals_send,
    totals_recv,
    sums_send,
    sums_recv,
    comp_send,
    comp_recv,
    scalar_sem,
    known_x,
    known_y,
):
    count = tiles_hbm.shape[0]
    blocks = disp_hbm.shape[0]
    nix = face_x_ref.shape[2]
    niy = face_y_ref.shape[2]
    gx = lax.axis_index("gx")
    gy = lax.axis_index("gy")

    barrier = pltpu.get_barrier_semaphore()

    def each_way(distance, body):
        for side, (place, size, where) in enumerate(
            ((gx, n_gx, lambda d: (gx + d, gy)), (gy, n_gy, lambda d: (gx, gy + d)))
        ):
            if distance < size:

                @pl.when(place + distance < size)
                def _(side=side, where=where):
                    body(side, 0, where(distance))

                @pl.when(place >= distance)
                def _(side=side, where=where):
                    body(side, 1, where(-distance))

    def greet(side, way, where):
        pl.semaphore_signal(barrier, inc=1, device_id=where, device_id_type=MESH)

    each_way(1, greet)

    loads = [
        pltpu.make_async_copy(src, dst, load_sem.at[k])
        for k, (src, dst) in enumerate(
            ((disp_hbm, disp_raw), (adj_hbm, adj_raw), (tiles_hbm, tiles_raw))
        )
    ]
    scalar_loads = [
        pltpu.make_async_copy(src, dst, scalar_sem.at[k])
        for k, (src, dst) in enumerate(
            (
                (face_x_hbm, face_x_ref),
                (face_y_hbm, face_y_ref),
                (rows_hbm, rows_ref),
                (cols_hbm, cols_ref),
                (density_hbm, density_ref),
                (weight_hbm, weight_ref),
                (owner_hbm, owner_ref),
                (region_hbm, region_ref),
            )
        )
    ]
    for load in loads[:2] + scalar_loads + loads[2:]:
        load.start()

    def learn_start(step):
        def body(side, way, where):
            known = known_x if side == 0 else known_y
            pl.semaphore_signal(
                known.at[step, way], inc=1, device_id=where, device_id_type=MESH
            )

        each_way(2**step, body)

    def learn_finish(step):
        def body(side, way, where):
            known = known_x if side == 0 else known_y
            pl.semaphore_wait(known.at[step, 1 - way], 1)

        each_way(2**step, body)

    steps = (max(n_gx, n_gy) - 1).bit_length()

    def widen(raw, wide, height):
        def read(c):
            at = pl.ds(pl.multiple_of(c * LANES, LANES), LANES)
            return raw[:, at].astype(F32)

        def write(c, chunk):
            wide[pl.ds(c * (height + 1), height), :] = chunk

        loop(HALF, 4, read, write)

    low_lanes = lax.broadcasted_iota(jnp.int32, (HALF, LANES), 1) < R

    loads[0].wait()
    widen(disp_raw, disp_wide, blocks)
    loads[1].wait()
    widen(adj_raw, adj_wide, blocks)

    def parts(b):
        u = disp_wide[pl.ds(b, HALF, stride=blocks + 1), :]
        a = adj_wide[pl.ds(b, HALF, stride=blocks + 1), :]
        u_turned = pltpu.roll(u, R, 1)
        a_turned = pltpu.roll(a, R, 1)
        even = jnp.where(low_lanes, a, u_turned)
        odd = jnp.where(low_lanes, a_turned, u)
        even_swapped = jnp.where(low_lanes, u, a_turned)
        odd_swapped = jnp.where(low_lanes, u_turned, a)
        block = jnp.concatenate([even, odd], axis=0).astype(BF16)
        swapped = jnp.concatenate([even_swapped, odd_swapped], axis=0).astype(BF16)
        return block, swapped

    def keep_local(b, pair):
        block, swapped = pair
        local[b, :, 0:LANES] = block
        local[b, :, LANES : 2 * LANES] = swapped
        ext[b] = block

    def stage(faces, way, at, number):
        def write(k, block):
            staged[at + k] = block

        loop(number, 4, lambda k: parts(faces[0, way, k])[0], write)

    first = blocks
    plans = (
        (0, first, nix, gx < n_gx - 1, (gx + 1, gy), gx > 0),
        (nix, first + nix, nix, gx > 0, (gx - 1, gy), gx < n_gx - 1),
        (2 * nix, first + 2 * nix, niy, gy < n_gy - 1, (gx, gy + 1), gy > 0),
        (2 * nix + niy, first + 2 * nix + niy, niy, gy > 0, (gx, gy - 1), gy < n_gy - 1),
    )

    def halo(k):
        at, to, number, _, where, _ = plans[k]
        return exchange(
            staged.at[pl.ds(at, number)],
            ext.at[pl.ds(to, number)],
            halo_send.at[k],
            halo_recv.at[k],
            where,
        )

    for load in scalar_loads[:2]:
        load.wait()
    for k, (at, to, number, has_target, _, has_source) in enumerate(plans):
        stage(face_x_ref if k < 2 else face_y_ref, k % 2, at, number)
        if k == 0:
            neighbours = (
                (gx > 0).astype(jnp.int32)
                + (gx < n_gx - 1).astype(jnp.int32)
                + (gy > 0).astype(jnp.int32)
                + (gy < n_gy - 1).astype(jnp.int32)
            )
            pl.semaphore_wait(barrier, neighbours)

        @pl.when(has_target)
        def _(k=k):
            halo(k).start()

        @pl.when(jnp.logical_not(has_source))
        def _(to=to, number=number):
            ext[pl.ds(to, number)] = jnp.zeros((number, BS, LANES), BF16)

    learn_start(0)
    loop(blocks, 4, parts, keep_local)
    learn_finish(0)
    for step in range(1, steps):
        learn_start(step)
        if step < steps - 1:
            learn_finish(step)
    for load in scalar_loads[2:]:
        load.wait()

    regions = n_gy * NREG
    key_lane = lax.broadcasted_iota(jnp.int32, (1, regions), 1)

    def key_row(t):
        key = owner_ref[t] * NREG + region_ref[t]
        return (key_lane == key).astype(F32), jnp.full((1, LANES), weight_ref[t], F32)

    def keep_key(t, rows):
        onehot[pl.ds(t, 1), :] = rows[0]
        weights[pl.ds(t, 1), :] = rows[1]

    loop(count, 8, key_row, keep_key)
    hot = onehot[...].astype(BF16)
    totals_out[...] = rows_by_region(hot, weights[...]).reshape(n_gy, NREG, LANES)
    totals_in[gy] = totals_out[gy]

    def totals_copy(j, slot):
        return exchange(
            totals_out.at[j], totals_in.at[slot], totals_send.at[j], totals_recv.at[slot], (gx, j)
        )

    def sums_copy(j, slot):
        return exchange(
            sums_out.at[j], sums_in.at[slot], sums_send.at[j], sums_recv.at[slot], (gx, j)
        )

    def comp_copy(i, slot):
        return exchange(comp_out, comp_in.at[slot], comp_send.at[i], comp_recv.at[slot], (i, gy))

    def others(size, me, body):
        @pl.loop(0, size)
        def _(i):
            @pl.when(i != me)
            def _():
                body(i)

    loads[2].wait()
    widen(tiles_raw, tiles_wide, count)

    def turn(i):
        t = 2 * i
        one = tiles_wide[pl.ds(t, HALF, stride=count + 1), :]
        two = tiles_wide[pl.ds(t + 1, HALF, stride=count + 1), :]
        even = jnp.where(low_lanes, one, pltpu.roll(two, BS, 1))
        odd = jnp.where(low_lanes, pltpu.roll(one, BS, 1), two)
        return jnp.concatenate([even, odd], axis=0).astype(BF16).T

    def keep_turned(i, value):
        turned[i] = value

    loop(count // 2, 4, turn, keep_turned)

    def product(t, i, k):
        return jnp.dot(
            turned[i, k * BS : (k + 1) * BS, :], local[rows_ref[t]], preferred_element_type=F32
        )

    def keep_product(t, result):
        at = pl.ds(pl.multiple_of(t * BS, BS), BS)
        prod[at, :] = result[:, 0:LANES]
        prod_swapped[at, :] = result[:, LANES : 2 * LANES]

    def product_pair(i):
        return product(2 * i, i, 0), product(2 * i + 1, i, 1)

    def keep_pair(i, results):
        keep_product(2 * i, results[0])
        keep_product(2 * i + 1, results[1])

    loop(count // 2, 2, product_pair, keep_pair)
    if steps > 1:
        learn_finish(steps - 1)
    others(n_gy, gy, lambda j: totals_copy(j, gy).start())

    for k, (_, _, _, _, _, has_source) in enumerate(plans):

        @pl.when(has_source)
        def _(k=k):
            halo(k).wait_recv()

    low8 = lax.broadcasted_iota(jnp.int32, (8, LANES), 1) < R

    def fold(x):
        parts = [x[8 * k : 8 * k + 8, :] for k in range(HALF // 8)]
        return (parts[0] + parts[1]) + (parts[2] + parts[3])

    def element(t):
        base = t * BS
        block = ext[cols_ref[t]]
        even = block[0:HALF, :].astype(F32)
        odd = block[HALF:BS, :].astype(F32)
        at_even = pl.ds(base, HALF, stride=2)
        at_odd = pl.ds(base + 1, HALF, stride=2)
        straight = fold(prod[at_even, :] * even + prod[at_odd, :] * odd)
        crossed = fold(prod_swapped[at_even, :] * even + prod_swapped[at_odd, :] * odd)
        cross = crossed + pltpu.roll(crossed, R, 1)
        strain = straight * (1.0 / math.sqrt(BS))
        rho = density_ref[t]
        sens = cross * (rho * rho * (-3.0 / (2.0 * math.sqrt(BS))))
        return weight_ref[t] * jnp.where(low8, sens, strain), strain

    unroll = 8

    def elements(i, total_energy):
        values = [element(i * unroll + k) for k in range(unroll)]
        for k, (value, strain) in enumerate(values):
            partial[pl.ds((i * unroll + k) * 9, 8), :] = value
            total_energy = total_energy + strain
        return total_energy

    comp = lax.fori_loop(0, count // unroll, elements, jnp.zeros((8, LANES), F32))

    payload = partial[pl.ds(0, count, stride=9), :]
    for s in range(1, 8):
        payload = payload + partial[pl.ds(s, count, stride=9), :]
    sums_out[:, 0:NREG, :] = rows_by_region(hot, payload).reshape(n_gy, NREG, LANES)
    for j in range(n_gy):
        sums_out[j, NREG : NREG + 8, :] = comp
    sums_in[gy] = sums_out[gy]
    others(n_gy, gy, lambda j: sums_copy(j, gy).start())
    others(n_gy, gy, lambda j: sums_copy(j, j).wait_recv())
    gathered = sums_in[0]
    for j in range(1, n_gy):
        gathered = gathered + sums_in[j]
    comp_out[...] = gathered[NREG : NREG + 8, :]
    comp_in[gx] = comp_out[...]
    others(n_gx, gx, lambda i: comp_copy(i, gx).start())
    others(n_gy, gy, lambda j: totals_copy(j, j).wait_recv())
    total = jnp.zeros((NREG, LANES), F32)
    for j in range(n_gy):
        total = total + totals_in[j]
    scale = 1.0 / jnp.maximum(total, 1.0)
    filtered_ref[...] = gathered[0:NREG, :] * scale

    for k, (_, _, _, has_target, _, _) in enumerate(plans):

        @pl.when(has_target)
        def _(k=k):
            halo(k).wait_send()

    others(n_gy, gy, lambda j: totals_copy(j, gy).wait_send())
    others(n_gy, gy, lambda j: sums_copy(j, gy).wait_send())

    others(n_gx, gx, lambda i: comp_copy(i, i).wait_recv())
    everything = lax.fori_loop(
        0, n_gx, lambda i, acc: acc + comp_in[i], jnp.zeros((8, LANES), F32)
    )
    line = jnp.sum(everything, axis=0, keepdims=True) / math.sqrt(count * n_gx * n_gy)
    turned_line = pltpu.roll(jnp.broadcast_to(line, (8, LANES)), R, 1)
    compliance_ref[...] = turned_line[0, 0:R]
    others(n_gx, gx, lambda i: comp_copy(i, gx).wait_send())


def shards(n_gx, n_gy, *args):
    (
        disp,
        adjoint,
        tiles,
        tile_rows,
        tile_cols,
        density,
        filter_weight,
        owner,
        region,
        face_x,
        face_y,
    ) = args
    count = tiles.shape[0]
    blocks = disp.shape[0]
    faces = face_x.shape[2] * 2 + face_y.shape[2] * 2
    hbm = pl.BlockSpec(memory_space=pltpu.HBM)
    steps = (max(n_gx, n_gy) - 1).bit_length()
    vmem = pl.BlockSpec(memory_space=pltpu.VMEM)
    dma = pltpu.SemaphoreType.DMA
    filtered, compliance = pl.pallas_call(
        functools.partial(kernel, n_gx, n_gy),
        out_shape=(
            jax.ShapeDtypeStruct((NREG, LANES), F32),
            jax.ShapeDtypeStruct((R,), F32),
        ),
        in_specs=[hbm] * 11,
        out_specs=(vmem, vmem),
        scratch_shapes=[
            *(pltpu.SMEM((count,), kind) for kind in (I32, I32, F32, F32, I32, I32)),
            pltpu.SMEM(face_x.shape, I32),
            pltpu.SMEM(face_y.shape, I32),
            pltpu.VMEM((blocks, BS * R), BF16),
            pltpu.VMEM((blocks, BS * R), BF16),
            pltpu.VMEM((count, BS * BS), BF16),
            pltpu.VMEM((HALF * (blocks + 1), LANES), F32),
            pltpu.VMEM((HALF * (blocks + 1), LANES), F32),
            pltpu.VMEM((HALF * (count + 1), LANES), F32),
            pltpu.VMEM((count // 2, 2 * BS, BS), BF16),
            pltpu.VMEM((blocks, BS, 2 * LANES), BF16),
            pltpu.VMEM((blocks + faces, BS, LANES), BF16),
            pltpu.VMEM((faces, BS, LANES), BF16),
            pltpu.VMEM((count * BS, LANES), F32),
            pltpu.VMEM((count * BS, LANES), F32),
            pltpu.VMEM((count, n_gy * NREG), F32),
            pltpu.VMEM((count, LANES), F32),
            pltpu.VMEM((count * 9, LANES), F32),
            pltpu.VMEM((8, LANES), F32),
            pltpu.VMEM((n_gy, NREG, LANES), F32),
            pltpu.VMEM((n_gy, NREG, LANES), F32),
            pltpu.VMEM((n_gy, NREG + 8, LANES), F32),
            pltpu.VMEM((n_gy, NREG + 8, LANES), F32),
            pltpu.VMEM((8, LANES), F32),
            pltpu.VMEM((n_gx, 8, LANES), F32),
            dma((3,)),
            dma((4,)),
            dma((4,)),
            dma((n_gy,)),
            dma((n_gy,)),
            dma((n_gy,)),
            dma((n_gy,)),
            dma((n_gx,)),
            dma((n_gx,)),
            dma((8,)),
            pltpu.SemaphoreType.REGULAR((steps, 2)),
            pltpu.SemaphoreType.REGULAR((steps, 2)),
        ],
        compiler_params=pltpu.CompilerParams(
            collective_id=0, has_side_effects=True, vmem_limit_bytes=40 * 2**20
        ),
        name="sensitivities",
    )(*[pltpu.with_memory_space_constraint(x, pltpu.HBM) for x in (
        tile_rows,
        tile_cols,
        density,
        filter_weight,
        owner.reshape(-1),
        region,
        face_x,
        face_y,
        disp,
        adjoint,
        tiles,
    )])
    return filtered, compliance


def solution(mesh):
    placed = (
        P(("gx", "gy"), None),
        P(("gx", "gy"), None),
        P(("gx", "gy"), None),
        P(("gx", "gy")),
        P(("gx", "gy")),
        P(("gx", "gy")),
        P(("gx", "gy")),
        P(("gx", "gy"), None),
        P(("gx", "gy")),
        P(("gx", "gy"), None, None),
        P(("gx", "gy"), None, None),
    )
    return jax.shard_map(
        functools.partial(shards, mesh.shape["gx"], mesh.shape["gy"]),
        mesh=mesh,
        in_specs=placed,
        out_specs=(P(("gx", "gy"), None), P()),
        check_vma=False,
    )
```

```python
import functools
import math

import jax
import jax.numpy as jnp
from jax import lax
from jax.experimental import pallas as pl
from jax.experimental.pallas import tpu as pltpu
from jax.sharding import PartitionSpec as P

BS = 64
R = 64
NREG = 32
LANES = 2 * R
HALF = BS // 2
MESH = pl.DeviceIdType.MESH
BF16 = jnp.bfloat16
F32 = jnp.float32
I32 = jnp.int32


def loop(count, unroll, read, write):
    def step(i, carry):
        places = [i * unroll + k for k in range(unroll)]
        values = [read(place) for place in places]
        for place, value in zip(places, values):
            write(place, value)
        return carry

    lax.fori_loop(0, count // unroll, step, 0)


def exchange(src, dst, send_sem, recv_sem, where):
    return pltpu.make_async_remote_copy(
        src_ref=src,
        dst_ref=dst,
        send_sem=send_sem,
        recv_sem=recv_sem,
        device_id=where,
        device_id_type=MESH,
    )


def two_terms(x):
    high = x.astype(BF16)
    low = (x - high.astype(F32)).astype(BF16)
    return jnp.concatenate([high, low], axis=0)


def rows_by_region(hot_turned, x):
    return jnp.dot(hot_turned, two_terms(x), preferred_element_type=F32)


def knowledge_rounds(n_gx, n_gy):
    return [
        (along, 2**step)
        for along, size in ((1, n_gy), (0, n_gx))
        for step in range((size - 1).bit_length())
    ]


def kernel(
    n_gx,
    n_gy,
    rows_hbm,
    cols_hbm,
    density_hbm,
    weight_hbm,
    owner_hbm,
    region_hbm,
    face_x_hbm,
    face_y_hbm,
    disp_hbm,
    adj_hbm,
    tiles_hbm,
    filtered_ref,
    compliance_ref,
    rows_ref,
    cols_ref,
    density_ref,
    weight_ref,
    owner_ref,
    region_ref,
    face_x_ref,
    face_y_ref,
    disp_raw,
    adj_raw,
    tiles_raw,
    disp_wide,
    adj_wide,
    tiles_wide,
    turned,
    local,
    ext,
    staged,
    prod,
    prod_swapped,
    onehot,
    hot_turned,
    weights,
    partial,
    totals_out,
    totals_in,
    sums_out,
    sums_in,
    comp_out,
    comp_in,
    load_sem,
    halo_send,
    halo_recv,
    totals_send,
    totals_recv,
    sums_send,
    sums_recv,
    comp_send,
    comp_recv,
    scalar_sem,
    known,
):
    rounds = knowledge_rounds(n_gx, n_gy)
    count = tiles_hbm.shape[0]
    blocks = disp_hbm.shape[0]
    nix = face_x_ref.shape[2]
    niy = face_y_ref.shape[2]
    gx = lax.axis_index("gx")
    gy = lax.axis_index("gy")

    barrier = pltpu.get_barrier_semaphore()

    def each_way(distance, body):
        for side, (place, size, where) in enumerate(
            ((gx, n_gx, lambda d: (gx + d, gy)), (gy, n_gy, lambda d: (gx, gy + d)))
        ):
            if distance < size:

                @pl.when(place + distance < size)
                def _(side=side, where=where):
                    body(side, 0, where(distance))

                @pl.when(place >= distance)
                def _(side=side, where=where):
                    body(side, 1, where(-distance))

    def greet(side, way, where):
        pl.semaphore_signal(barrier, inc=1, device_id=where, device_id_type=MESH)

    each_way(1, greet)

    loads = [
        pltpu.make_async_copy(src, dst, load_sem.at[k])
        for k, (src, dst) in enumerate(
            ((disp_hbm, disp_raw), (adj_hbm, adj_raw), (tiles_hbm, tiles_raw))
        )
    ]
    scalar_loads = [
        pltpu.make_async_copy(src, dst, scalar_sem.at[k])
        for k, (src, dst) in enumerate(
            (
                (face_x_hbm, face_x_ref),
                (face_y_hbm, face_y_ref),
                (rows_hbm, rows_ref),
                (cols_hbm, cols_ref),
                (density_hbm, density_ref),
                (weight_hbm, weight_ref),
                (owner_hbm, owner_ref),
                (region_hbm, region_ref),
            )
        )
    ]
    for load in loads[:2] + scalar_loads + loads[2:]:
        load.start()

    def learn(step, act):
        along, distance = rounds[step]

        def body(side, way, where):
            if side == along:
                act(step, way, where)

        each_way(distance, body)

    def tell(step, way, where):
        pl.semaphore_signal(known.at[step, way], inc=1, device_id=where, device_id_type=MESH)

    def hear(step, way, where):
        pl.semaphore_wait(known.at[step, 1 - way], 1)

    def next_round(step):
        if step > 0:
            learn(step - 1, hear)
        if step < len(rounds):
            learn(step, tell)

    def widen(raw, wide, height):
        def read(c):
            at = pl.ds(pl.multiple_of(c * LANES, LANES), LANES)
            return raw[:, at].astype(F32)

        def write(c, chunk):
            wide[pl.ds(c * (height + 1), height), :] = chunk

        loop(HALF, 4, read, write)

    low_lanes = lax.broadcasted_iota(jnp.int32, (HALF, LANES), 1) < R

    loads[0].wait()
    widen(disp_raw, disp_wide, blocks)
    loads[1].wait()
    widen(adj_raw, adj_wide, blocks)

    def parts(b):
        u = disp_wide[pl.ds(b, HALF, stride=blocks + 1), :]
        a = adj_wide[pl.ds(b, HALF, stride=blocks + 1), :]
        u_turned = pltpu.roll(u, R, 1)
        a_turned = pltpu.roll(a, R, 1)
        even = jnp.where(low_lanes, a, u_turned)
        odd = jnp.where(low_lanes, a_turned, u)
        even_swapped = jnp.where(low_lanes, u, a_turned)
        odd_swapped = jnp.where(low_lanes, u_turned, a)
        block = jnp.concatenate([even, odd], axis=0).astype(BF16)
        swapped = jnp.concatenate([even_swapped, odd_swapped], axis=0).astype(BF16)
        return block, swapped

    def keep_local(b, pair):
        block, swapped = pair
        local[b, :, 0:LANES] = block
        local[b, :, LANES : 2 * LANES] = swapped
        ext[b] = block

    def stage(faces, way, at, number):
        def write(k, block):
            staged[at + k] = block

        loop(number, 4, lambda k: parts(faces[0, way, k])[0], write)

    first = blocks
    plans = (
        (0, first, nix, gx < n_gx - 1, (gx + 1, gy), gx > 0),
        (nix, first + nix, nix, gx > 0, (gx - 1, gy), gx < n_gx - 1),
        (2 * nix, first + 2 * nix, niy, gy < n_gy - 1, (gx, gy + 1), gy > 0),
        (2 * nix + niy, first + 2 * nix + niy, niy, gy > 0, (gx, gy - 1), gy < n_gy - 1),
    )

    def halo(k):
        at, to, number, _, where, _ = plans[k]
        return exchange(
            staged.at[pl.ds(at, number)],
            ext.at[pl.ds(to, number)],
            halo_send.at[k],
            halo_recv.at[k],
            where,
        )

    for load in scalar_loads[:2]:
        load.wait()
    for k in (1, 0, 2, 3):
        at, to, number, has_target, _, has_source = plans[k]
        stage(face_x_ref if k < 2 else face_y_ref, k % 2, at, number)
        if k == 1:
            neighbours = (
                (gx > 0).astype(jnp.int32)
                + (gx < n_gx - 1).astype(jnp.int32)
                + (gy > 0).astype(jnp.int32)
                + (gy < n_gy - 1).astype(jnp.int32)
            )
            pl.semaphore_wait(barrier, neighbours)

        @pl.when(has_target)
        def _(k=k):
            halo(k).start()

        @pl.when(jnp.logical_not(has_source))
        def _(to=to, number=number):
            ext[pl.ds(to, number)] = jnp.zeros((number, BS, LANES), BF16)

        if k == 1:
            next_round(0)

    loop(blocks, 4, parts, keep_local)
    next_round(1)
    for load in scalar_loads[2:]:
        load.wait()

    regions = n_gy * NREG
    key_lane = lax.broadcasted_iota(jnp.int32, (1, regions), 1)

    def key_row(t):
        key = owner_ref[t] * NREG + region_ref[t]
        return (key_lane == key).astype(F32), jnp.full((1, LANES), weight_ref[t], F32)

    def keep_key(t, rows):
        onehot[pl.ds(t, 1), :] = rows[0]
        weights[pl.ds(t, 1), :] = rows[1]

    loop(count, 8, key_row, keep_key)
    hot = onehot[...].astype(BF16)
    hot_turned[...] = jnp.concatenate([hot, hot], axis=0).T
    totals_out[...] = rows_by_region(hot_turned[...], weights[...]).reshape(n_gy, NREG, LANES)
    totals_in[gy] = totals_out[gy]
    next_round(2)

    def totals_copy(j, slot):
        return exchange(
            totals_out.at[j], totals_in.at[slot], totals_send.at[j], totals_recv.at[slot], (gx, j)
        )

    def sums_copy(j, slot):
        return exchange(
            sums_out.at[j], sums_in.at[slot], sums_send.at[j], sums_recv.at[slot], (gx, j)
        )

    me = gx * n_gy + gy

    def comp_copy(d, slot):
        return exchange(
            comp_out,
            comp_in.at[slot],
            comp_send.at[d],
            comp_recv.at[slot],
            (lax.div(d, n_gy), lax.rem(d, n_gy)),
        )

    def others(size, own, body):
        @pl.loop(1, size)
        def _(offset):
            body(lax.rem(own + offset, size))

    loads[2].wait()
    widen(tiles_raw, tiles_wide, count)

    def turn(i):
        t = 2 * i
        one = tiles_wide[pl.ds(t, HALF, stride=count + 1), :]
        two = tiles_wide[pl.ds(t + 1, HALF, stride=count + 1), :]
        even = jnp.where(low_lanes, one, pltpu.roll(two, BS, 1))
        odd = jnp.where(low_lanes, pltpu.roll(one, BS, 1), two)
        return jnp.concatenate([even, odd], axis=0).astype(BF16).T

    def keep_turned(i, value):
        turned[i] = value

    loop(count // 2, 4, turn, keep_turned)
    next_round(3)

    def product(t, i, k):
        return jnp.dot(
            turned[i, k * BS : (k + 1) * BS, :], local[rows_ref[t]], preferred_element_type=F32
        )

    def keep_product(t, result):
        at = pl.ds(pl.multiple_of(t * BS, BS), BS)
        prod[at, :] = result[:, 0:LANES]
        prod_swapped[at, :] = result[:, LANES : 2 * LANES]

    def product_pair(i):
        return product(2 * i, i, 0), product(2 * i + 1, i, 1)

    def keep_pair(i, results):
        keep_product(2 * i, results[0])
        keep_product(2 * i + 1, results[1])

    loop(count // 2, 4, product_pair, keep_pair)
    for step in range(4, len(rounds)):
        next_round(step)
    others(n_gy, gy, lambda j: totals_copy(j, gy).start())

    for k, (_, _, _, _, _, has_source) in enumerate(plans):

        @pl.when(has_source)
        def _(k=k):
            halo(k).wait_recv()

    low8 = lax.broadcasted_iota(jnp.int32, (8, LANES), 1) < R

    def fold(x):
        parts = [x[8 * k : 8 * k + 8, :] for k in range(HALF // 8)]
        return (parts[0] + parts[1]) + (parts[2] + parts[3])

    def element(t):
        base = t * BS
        block = ext[cols_ref[t]]
        even = block[0:HALF, :].astype(F32)
        odd = block[HALF:BS, :].astype(F32)
        at_even = pl.ds(base, HALF, stride=2)
        at_odd = pl.ds(base + 1, HALF, stride=2)
        straight = fold(prod[at_even, :] * even + prod[at_odd, :] * odd)
        crossed = fold(prod_swapped[at_even, :] * even + prod_swapped[at_odd, :] * odd)
        cross = crossed + pltpu.roll(crossed, R, 1)
        strain = straight * (1.0 / math.sqrt(BS))
        rho = density_ref[t]
        sens = cross * (rho * rho * (-3.0 / (2.0 * math.sqrt(BS))))
        return weight_ref[t] * jnp.where(low8, sens, strain), strain

    unroll = 8

    def elements(i, total_energy):
        values = [element(i * unroll + k) for k in range(unroll)]
        for k, (value, strain) in enumerate(values):
            partial[pl.ds((i * unroll + k) * 9, 8), :] = value
            total_energy = total_energy + strain
        return total_energy

    comp = lax.fori_loop(0, count // unroll, elements, jnp.zeros((8, LANES), F32))

    next_round(len(rounds))
    comp_out[...] = jnp.sum(comp, axis=0, keepdims=True)
    comp_in[me] = comp_out[...]
    others(n_gx * n_gy, me, lambda d: comp_copy(d, me).start())

    payload = partial[pl.ds(0, count, stride=9), :]
    for s in range(1, 8):
        payload = payload + partial[pl.ds(s, count, stride=9), :]
    sums_out[...] = rows_by_region(hot_turned[...], payload).reshape(n_gy, NREG, LANES)
    sums_in[gy] = sums_out[gy]
    others(n_gy, gy, lambda j: sums_copy(j, gy).start())

    for k, (_, _, _, has_target, _, _) in enumerate(plans):

        @pl.when(has_target)
        def _(k=k):
            halo(k).wait_send()

    others(n_gy, gy, lambda j: totals_copy(j, gy).wait_send())
    others(n_gy, gy, lambda j: totals_copy(j, j).wait_recv())
    total = jnp.zeros((NREG, LANES), F32)
    for j in range(n_gy):
        total = total + totals_in[j]
    scale = 1.0 / jnp.maximum(total, 1.0)
    others(n_gx * n_gy, me, lambda d: comp_copy(d, me).wait_send())

    others(n_gy, gy, lambda j: sums_copy(j, gy).wait_send())
    others(n_gy, gy, lambda j: sums_copy(j, j).wait_recv())
    gathered = sums_in[0]
    for j in range(1, n_gy):
        gathered = gathered + sums_in[j]
    filtered_ref[...] = gathered * scale

    others(n_gx * n_gy, me, lambda d: comp_copy(d, d).wait_recv())
    unroll = n_gy

    def gather(i, acc):
        for k in range(unroll):
            acc = acc + comp_in[i * unroll + k]
        return acc

    line = lax.fori_loop(0, n_gx, gather, jnp.zeros((1, LANES), F32))
    line = line * (1.0 / math.sqrt(count * n_gx * n_gy))
    turned_line = pltpu.roll(jnp.broadcast_to(line, (8, LANES)), R, 1)
    compliance_ref[...] = turned_line[0, 0:R]


def shards(n_gx, n_gy, *args):
    (
        disp,
        adjoint,
        tiles,
        tile_rows,
        tile_cols,
        density,
        filter_weight,
        owner,
        region,
        face_x,
        face_y,
    ) = args
    count = tiles.shape[0]
    blocks = disp.shape[0]
    faces = face_x.shape[2] * 2 + face_y.shape[2] * 2
    hbm = pl.BlockSpec(memory_space=pltpu.HBM)
    vmem = pl.BlockSpec(memory_space=pltpu.VMEM)
    dma = pltpu.SemaphoreType.DMA
    filtered, compliance = pl.pallas_call(
        functools.partial(kernel, n_gx, n_gy),
        out_shape=(
            jax.ShapeDtypeStruct((NREG, LANES), F32),
            jax.ShapeDtypeStruct((R,), F32),
        ),
        in_specs=[hbm] * 11,
        out_specs=(vmem, vmem),
        scratch_shapes=[
            *(pltpu.SMEM((count,), kind) for kind in (I32, I32, F32, F32, I32, I32)),
            pltpu.SMEM(face_x.shape, I32),
            pltpu.SMEM(face_y.shape, I32),
            pltpu.VMEM((blocks, BS * R), BF16),
            pltpu.VMEM((blocks, BS * R), BF16),
            pltpu.VMEM((count, BS * BS), BF16),
            pltpu.VMEM((HALF * (blocks + 1), LANES), F32),
            pltpu.VMEM((HALF * (blocks + 1), LANES), F32),
            pltpu.VMEM((HALF * (count + 1), LANES), F32),
            pltpu.VMEM((count // 2, 2 * BS, BS), BF16),
            pltpu.VMEM((blocks, BS, 2 * LANES), BF16),
            pltpu.VMEM((blocks + faces, BS, LANES), BF16),
            pltpu.VMEM((faces, BS, LANES), BF16),
            pltpu.VMEM((count * BS, LANES), F32),
            pltpu.VMEM((count * BS, LANES), F32),
            pltpu.VMEM((count, n_gy * NREG), F32),
            pltpu.VMEM((n_gy * NREG, 2 * count), BF16),
            pltpu.VMEM((count, LANES), F32),
            pltpu.VMEM((count * 9, LANES), F32),
            *[pltpu.VMEM((n_gy, NREG, LANES), F32)] * 4,
            pltpu.VMEM((1, LANES), F32),
            pltpu.VMEM((n_gx * n_gy, 1, LANES), F32),
            dma((3,)),
            dma((4,)),
            dma((4,)),
            dma((n_gy,)),
            dma((n_gy,)),
            dma((n_gy,)),
            dma((n_gy,)),
            dma((n_gx * n_gy,)),
            dma((n_gx * n_gy,)),
            dma((8,)),
            pltpu.SemaphoreType.REGULAR((len(knowledge_rounds(n_gx, n_gy)), 2)),
        ],
        compiler_params=pltpu.CompilerParams(
            collective_id=0, has_side_effects=True, vmem_limit_bytes=40 * 2**20
        ),
        name="sensitivities",
    )(*[pltpu.with_memory_space_constraint(x, pltpu.HBM) for x in (
        tile_rows,
        tile_cols,
        density,
        filter_weight,
        owner.reshape(-1),
        region,
        face_x,
        face_y,
        disp,
        adjoint,
        tiles,
    )])
    return filtered, compliance


def solution(mesh):
    placed = (
        P(("gx", "gy"), None),
        P(("gx", "gy"), None),
        P(("gx", "gy"), None),
        P(("gx", "gy")),
        P(("gx", "gy")),
        P(("gx", "gy")),
        P(("gx", "gy")),
        P(("gx", "gy"), None),
        P(("gx", "gy")),
        P(("gx", "gy"), None, None),
        P(("gx", "gy"), None, None),
    )
    return jax.shard_map(
        functools.partial(shards, mesh.shape["gx"], mesh.shape["gy"]),
        mesh=mesh,
        in_specs=placed,
        out_specs=(P(("gx", "gy"), None), P()),
        check_vma=False,
    )
```

```python
import functools
import math

import jax
import jax.numpy as jnp
from jax import lax
from jax.experimental import pallas as pl
from jax.experimental.pallas import tpu as pltpu
from jax.sharding import PartitionSpec as P

BS = 64
R = 64
NREG = 32
LANES = 2 * R
HALF = BS // 2
MESH = pl.DeviceIdType.MESH
BF16 = jnp.bfloat16
F32 = jnp.float32
I32 = jnp.int32


def loop(count, unroll, read, write):
    def step(i, carry):
        places = [i * unroll + k for k in range(unroll)]
        values = [read(place) for place in places]
        for place, value in zip(places, values):
            write(place, value)
        return carry

    lax.fori_loop(0, count // unroll, step, 0)


def exchange(src, dst, send_sem, recv_sem, where):
    return pltpu.make_async_remote_copy(
        src_ref=src,
        dst_ref=dst,
        send_sem=send_sem,
        recv_sem=recv_sem,
        device_id=where,
        device_id_type=MESH,
    )


def two_terms(x):
    high = x.astype(BF16)
    low = (x - high.astype(F32)).astype(BF16)
    return jnp.concatenate([high, low], axis=0)


def rows_by_region(hot_turned, x):
    return jnp.dot(hot_turned, two_terms(x), preferred_element_type=F32)


def knowledge_rounds(n_gx, n_gy):
    return [
        (along, 2**step)
        for along, size in ((1, n_gy), (0, n_gx))
        for step in range((size - 1).bit_length())
    ]


def kernel(
    n_gx,
    n_gy,
    rows_hbm,
    cols_hbm,
    density_hbm,
    weight_hbm,
    owner_hbm,
    region_hbm,
    face_x_hbm,
    face_y_hbm,
    disp_hbm,
    adj_hbm,
    tiles_hbm,
    filtered_ref,
    compliance_ref,
    rows_ref,
    cols_ref,
    density_ref,
    weight_ref,
    owner_ref,
    region_ref,
    face_x_ref,
    face_y_ref,
    disp_raw,
    adj_raw,
    tiles_raw,
    disp_wide,
    adj_wide,
    tiles_wide,
    turned,
    local,
    ext,
    staged,
    prod,
    prod_swapped,
    onehot,
    hot_turned,
    weights,
    partial,
    totals_out,
    totals_in,
    sums_out,
    sums_in,
    comp_out,
    comp_in,
    load_sem,
    halo_send,
    halo_recv,
    totals_send,
    totals_recv,
    sums_send,
    sums_recv,
    comp_send,
    comp_recv,
    scalar_sem,
    known,
):
    rounds = knowledge_rounds(n_gx, n_gy)
    count = tiles_hbm.shape[0]
    blocks = disp_hbm.shape[0]
    nix = face_x_ref.shape[2]
    niy = face_y_ref.shape[2]
    gx = lax.axis_index("gx")
    gy = lax.axis_index("gy")

    barrier = pltpu.get_barrier_semaphore()

    def each_way(distance, body):
        for side, (place, size, where) in enumerate(
            ((gx, n_gx, lambda d: (gx + d, gy)), (gy, n_gy, lambda d: (gx, gy + d)))
        ):
            if distance < size:

                @pl.when(place + distance < size)
                def _(side=side, where=where):
                    body(side, 0, where(distance))

                @pl.when(place >= distance)
                def _(side=side, where=where):
                    body(side, 1, where(-distance))

    def greet(side, way, where):
        pl.semaphore_signal(barrier, inc=1, device_id=where, device_id_type=MESH)

    each_way(1, greet)

    loads = [
        pltpu.make_async_copy(src, dst, load_sem.at[k])
        for k, (src, dst) in enumerate(
            ((disp_hbm, disp_raw), (adj_hbm, adj_raw), (tiles_hbm, tiles_raw))
        )
    ]
    scalar_loads = [
        pltpu.make_async_copy(src, dst, scalar_sem.at[k])
        for k, (src, dst) in enumerate(
            (
                (face_x_hbm, face_x_ref),
                (face_y_hbm, face_y_ref),
                (rows_hbm, rows_ref),
                (cols_hbm, cols_ref),
                (density_hbm, density_ref),
                (weight_hbm, weight_ref),
                (owner_hbm, owner_ref),
                (region_hbm, region_ref),
            )
        )
    ]
    for load in scalar_loads[5:] + loads[:2] + scalar_loads[:5] + loads[2:]:
        load.start()

    def learn(step, act):
        along, distance = rounds[step]

        def body(side, way, where):
            if side == along:
                act(step, way, where)

        each_way(distance, body)

    def tell(step, way, where):
        pl.semaphore_signal(known.at[step, way], inc=1, device_id=where, device_id_type=MESH)

    def hear(step, way, where):
        pl.semaphore_wait(known.at[step, 1 - way], 1)

    def next_round(step):
        if step > 0:
            learn(step - 1, hear)
        if step < len(rounds):
            learn(step, tell)

    def widen(raw, wide, height):
        def read(c):
            at = pl.ds(pl.multiple_of(c * LANES, LANES), LANES)
            return raw[:, at].astype(F32)

        def write(c, chunk):
            wide[pl.ds(c * (height + 1), height), :] = chunk

        loop(HALF, 4, read, write)

    low_lanes = lax.broadcasted_iota(jnp.int32, (HALF, LANES), 1) < R

    for load in scalar_loads[5:]:
        load.wait()
    regions = n_gy * NREG
    key_lane = lax.broadcasted_iota(jnp.int32, (1, regions), 1)

    def key_row(t):
        key = owner_ref[t] * NREG + region_ref[t]
        return (key_lane == key).astype(F32), jnp.full((1, LANES), weight_ref[t], F32)

    def keep_key(t, rows):
        onehot[pl.ds(t, 1), :] = rows[0]
        weights[pl.ds(t, 1), :] = rows[1]

    loop(count, 8, key_row, keep_key)

    loads[0].wait()
    widen(disp_raw, disp_wide, blocks)
    loads[1].wait()
    widen(adj_raw, adj_wide, blocks)

    def parts(b):
        u = disp_wide[pl.ds(b, HALF, stride=blocks + 1), :]
        a = adj_wide[pl.ds(b, HALF, stride=blocks + 1), :]
        u_turned = pltpu.roll(u, R, 1)
        a_turned = pltpu.roll(a, R, 1)
        even = jnp.where(low_lanes, a, u_turned)
        odd = jnp.where(low_lanes, a_turned, u)
        even_swapped = jnp.where(low_lanes, u, a_turned)
        odd_swapped = jnp.where(low_lanes, u_turned, a)
        block = jnp.concatenate([even, odd], axis=0).astype(BF16)
        swapped = jnp.concatenate([even_swapped, odd_swapped], axis=0).astype(BF16)
        return block, swapped

    def keep_local(b, pair):
        block, swapped = pair
        local[b, :, 0:LANES] = block
        local[b, :, LANES : 2 * LANES] = swapped
        ext[b] = block

    def stage(faces, way, at, number):
        def write(k, block):
            staged[at + k] = block

        loop(number, 4, lambda k: parts(faces[0, way, k])[0], write)

    first = blocks
    plans = (
        (0, first, nix, gx < n_gx - 1, (gx + 1, gy), gx > 0),
        (nix, first + nix, nix, gx > 0, (gx - 1, gy), gx < n_gx - 1),
        (2 * nix, first + 2 * nix, niy, gy < n_gy - 1, (gx, gy + 1), gy > 0),
        (2 * nix + niy, first + 2 * nix + niy, niy, gy > 0, (gx, gy - 1), gy < n_gy - 1),
    )

    def halo(k):
        at, to, number, _, where, _ = plans[k]
        return exchange(
            staged.at[pl.ds(at, number)],
            ext.at[pl.ds(to, number)],
            halo_send.at[k],
            halo_recv.at[k],
            where,
        )

    for load in scalar_loads[:2]:
        load.wait()
    for k in (1, 0, 3, 2):
        at, _, number, has_target, _, _ = plans[k]

        @pl.when(has_target)
        def _(k=k, at=at, number=number):
            stage(face_x_ref if k < 2 else face_y_ref, k % 2, at, number)

    neighbours = (
        (gx > 0).astype(jnp.int32)
        + (gx < n_gx - 1).astype(jnp.int32)
        + (gy > 0).astype(jnp.int32)
        + (gy < n_gy - 1).astype(jnp.int32)
    )
    pl.semaphore_wait(barrier, neighbours)
    for k in (1, 0, 3, 2):
        _, to, number, has_target, _, has_source = plans[k]

        @pl.when(has_target)
        def _(k=k):
            halo(k).start()

        @pl.when(jnp.logical_not(has_source))
        def _(to=to, number=number):
            ext[pl.ds(to, number)] = jnp.zeros((number, BS, LANES), BF16)

    next_round(0)
    loop(blocks, 4, parts, keep_local)
    next_round(1)
    for load in scalar_loads[2:5]:
        load.wait()

    hot = onehot[...].astype(BF16)
    hot_turned[...] = jnp.concatenate([hot, hot], axis=0).T
    totals_out[...] = rows_by_region(hot_turned[...], weights[...]).reshape(n_gy, NREG, LANES)
    totals_in[gy] = totals_out[gy]
    next_round(2)

    def totals_copy(j, slot):
        return exchange(
            totals_out.at[j], totals_in.at[slot], totals_send.at[j], totals_recv.at[slot], (gx, j)
        )

    def sums_copy(j, slot):
        return exchange(
            sums_out.at[j], sums_in.at[slot], sums_send.at[j], sums_recv.at[slot], (gx, j)
        )

    me = gx * n_gy + gy

    def comp_copy(d, slot):
        return exchange(
            comp_out,
            comp_in.at[slot],
            comp_send,
            comp_recv,
            (lax.div(d, n_gy), lax.rem(d, n_gy)),
        )

    def all_rows(sem):
        rows = comp_in.at[pl.ds(0, n_gx * n_gy - 1)]
        return pltpu.make_async_copy(rows, rows, sem)

    def others(size, own, body):
        @pl.loop(1, size)
        def _(offset):
            body(lax.rem(own + offset, size))

    loads[2].wait()
    widen(tiles_raw, tiles_wide, count)

    def turn(i):
        t = 2 * i
        one = tiles_wide[pl.ds(t, HALF, stride=count + 1), :]
        two = tiles_wide[pl.ds(t + 1, HALF, stride=count + 1), :]
        even = jnp.where(low_lanes, one, pltpu.roll(two, BS, 1))
        odd = jnp.where(low_lanes, pltpu.roll(one, BS, 1), two)
        return jnp.concatenate([even, odd], axis=0).astype(BF16).T

    def keep_turned(i, value):
        turned[i] = value

    loop(count // 2, 4, turn, keep_turned)
    next_round(3)

    def product(t, i, k):
        return jnp.dot(
            turned[i, k * BS : (k + 1) * BS, :], local[rows_ref[t]], preferred_element_type=F32
        )

    def keep_product(t, result):
        at = pl.ds(pl.multiple_of(t * BS, BS), BS)
        prod[at, :] = result[:, 0:LANES]
        prod_swapped[at, :] = result[:, LANES : 2 * LANES]

    def product_pair(i):
        return product(2 * i, i, 0), product(2 * i + 1, i, 1)

    def keep_pair(i, results):
        keep_product(2 * i, results[0])
        keep_product(2 * i + 1, results[1])

    loop(count // 2, 4, product_pair, keep_pair)
    for step in range(4, len(rounds)):
        next_round(step)
    others(n_gy, gy, lambda j: totals_copy(j, gy).start())

    for k, (_, _, _, _, _, has_source) in enumerate(plans):

        @pl.when(has_source)
        def _(k=k):
            halo(k).wait_recv()

    low8 = lax.broadcasted_iota(jnp.int32, (8, LANES), 1) < R

    def fold(x):
        parts = [x[8 * k : 8 * k + 8, :] for k in range(HALF // 8)]
        return (parts[0] + parts[1]) + (parts[2] + parts[3])

    def element(t):
        base = t * BS
        block = ext[cols_ref[t]]
        even = block[0:HALF, :].astype(F32)
        odd = block[HALF:BS, :].astype(F32)
        at_even = pl.ds(base, HALF, stride=2)
        at_odd = pl.ds(base + 1, HALF, stride=2)
        straight = fold(prod[at_even, :] * even + prod[at_odd, :] * odd)
        crossed = fold(prod_swapped[at_even, :] * even + prod_swapped[at_odd, :] * odd)
        cross = crossed + pltpu.roll(crossed, R, 1)
        strain = straight * (1.0 / math.sqrt(BS))
        rho = density_ref[t]
        sens = cross * (rho * rho * (-3.0 / (2.0 * math.sqrt(BS))))
        return weight_ref[t] * jnp.where(low8, sens, strain), strain

    unroll = 8

    def elements(i, total_energy):
        values = [element(i * unroll + k) for k in range(unroll)]
        for k, (value, strain) in enumerate(values):
            partial[pl.ds((i * unroll + k) * 9, 8), :] = value
            total_energy = total_energy + strain
        return total_energy

    comp = lax.fori_loop(0, count // unroll, elements, jnp.zeros((8, LANES), F32))

    next_round(len(rounds))
    comp_out[...] = jnp.sum(comp, axis=0, keepdims=True)
    comp_in[me] = comp_out[...]
    others(n_gx * n_gy, me, lambda d: comp_copy(d, me).start())

    payload = partial[pl.ds(0, count, stride=9), :]
    for s in range(1, 8):
        payload = payload + partial[pl.ds(s, count, stride=9), :]
    sums_out[...] = rows_by_region(hot_turned[...], payload).reshape(n_gy, NREG, LANES)
    sums_in[gy] = sums_out[gy]
    others(n_gy, gy, lambda j: sums_copy(j, gy).start())

    for k, (_, _, _, has_target, _, _) in enumerate(plans):

        @pl.when(has_target)
        def _(k=k):
            halo(k).wait_send()

    others(n_gy, gy, lambda j: totals_copy(j, gy).wait_send())
    others(n_gy, gy, lambda j: totals_copy(j, j).wait_recv())
    total = jnp.zeros((NREG, LANES), F32)
    for j in range(n_gy):
        total = total + totals_in[j]
    scale = 1.0 / jnp.maximum(total, 1.0)
    all_rows(comp_send).wait()

    others(n_gy, gy, lambda j: sums_copy(j, gy).wait_send())
    others(n_gy, gy, lambda j: sums_copy(j, j).wait_recv())
    gathered = sums_in[0]
    for j in range(1, n_gy):
        gathered = gathered + sums_in[j]
    filtered_ref[...] = gathered * scale

    all_rows(comp_recv).wait()
    unroll = n_gy

    def gather(i, acc):
        for k in range(unroll):
            acc = acc + comp_in[i * unroll + k]
        return acc

    line = lax.fori_loop(0, n_gx, gather, jnp.zeros((1, LANES), F32))
    line = line * (1.0 / math.sqrt(count * n_gx * n_gy))
    turned_line = pltpu.roll(jnp.broadcast_to(line, (8, LANES)), R, 1)
    compliance_ref[...] = turned_line[0, 0:R]


def shards(n_gx, n_gy, *args):
    (
        disp,
        adjoint,
        tiles,
        tile_rows,
        tile_cols,
        density,
        filter_weight,
        owner,
        region,
        face_x,
        face_y,
    ) = args
    count = tiles.shape[0]
    blocks = disp.shape[0]
    faces = face_x.shape[2] * 2 + face_y.shape[2] * 2
    hbm = pl.BlockSpec(memory_space=pltpu.HBM)
    vmem = pl.BlockSpec(memory_space=pltpu.VMEM)
    dma = pltpu.SemaphoreType.DMA
    filtered, compliance = pl.pallas_call(
        functools.partial(kernel, n_gx, n_gy),
        out_shape=(
            jax.ShapeDtypeStruct((NREG, LANES), F32),
            jax.ShapeDtypeStruct((R,), F32),
        ),
        in_specs=[hbm] * 11,
        out_specs=(vmem, vmem),
        scratch_shapes=[
            *(pltpu.SMEM((count,), kind) for kind in (I32, I32, F32, F32, I32, I32)),
            pltpu.SMEM(face_x.shape, I32),
            pltpu.SMEM(face_y.shape, I32),
            pltpu.VMEM((blocks, BS * R), BF16),
            pltpu.VMEM((blocks, BS * R), BF16),
            pltpu.VMEM((count, BS * BS), BF16),
            pltpu.VMEM((HALF * (blocks + 1), LANES), F32),
            pltpu.VMEM((HALF * (blocks + 1), LANES), F32),
            pltpu.VMEM((HALF * (count + 1), LANES), F32),
            pltpu.VMEM((count // 2, 2 * BS, BS), BF16),
            pltpu.VMEM((blocks, BS, 2 * LANES), BF16),
            pltpu.VMEM((blocks + faces, BS, LANES), BF16),
            pltpu.VMEM((faces, BS, LANES), BF16),
            pltpu.VMEM((count * BS, LANES), F32),
            pltpu.VMEM((count * BS, LANES), F32),
            pltpu.VMEM((count, n_gy * NREG), F32),
            pltpu.VMEM((n_gy * NREG, 2 * count), BF16),
            pltpu.VMEM((count, LANES), F32),
            pltpu.VMEM((count * 9, LANES), F32),
            *[pltpu.VMEM((n_gy, NREG, LANES), F32)] * 4,
            pltpu.VMEM((1, LANES), F32),
            pltpu.VMEM((n_gx * n_gy, 1, LANES), F32),
            dma((3,)),
            dma((4,)),
            dma((4,)),
            dma((n_gy,)),
            dma((n_gy,)),
            dma((n_gy,)),
            dma((n_gy,)),
            dma,
            dma,
            dma((8,)),
            pltpu.SemaphoreType.REGULAR((len(knowledge_rounds(n_gx, n_gy)), 2)),
        ],
        compiler_params=pltpu.CompilerParams(
            collective_id=0, has_side_effects=True, vmem_limit_bytes=40 * 2**20
        ),
        name="sensitivities",
    )(*[pltpu.with_memory_space_constraint(x, pltpu.HBM) for x in (
        tile_rows,
        tile_cols,
        density,
        filter_weight,
        owner.reshape(-1),
        region,
        face_x,
        face_y,
        disp,
        adjoint,
        tiles,
    )])
    return filtered, compliance


def solution(mesh):
    placed = (
        P(("gx", "gy"), None),
        P(("gx", "gy"), None),
        P(("gx", "gy"), None),
        P(("gx", "gy")),
        P(("gx", "gy")),
        P(("gx", "gy")),
        P(("gx", "gy")),
        P(("gx", "gy"), None),
        P(("gx", "gy")),
        P(("gx", "gy"), None, None),
        P(("gx", "gy"), None, None),
    )
    return jax.shard_map(
        functools.partial(shards, mesh.shape["gx"], mesh.shape["gy"]),
        mesh=mesh,
        in_specs=placed,
        out_specs=(P(("gx", "gy"), None), P()),
        check_vma=False,
    )
```

```python
import functools
import math

import jax
import jax.numpy as jnp
from jax import lax
from jax.experimental import pallas as pl
from jax.experimental.pallas import tpu as pltpu
from jax.sharding import PartitionSpec as P

BS = 64
R = 64
NREG = 32
LANES = 2 * R
HALF = BS // 2
MESH = pl.DeviceIdType.MESH
BF16 = jnp.bfloat16
F32 = jnp.float32
I32 = jnp.int32


def loop(count, unroll, read, write):
    def step(i, carry):
        places = [i * unroll + k for k in range(unroll)]
        values = [read(place) for place in places]
        for place, value in zip(places, values):
            write(place, value)
        return carry

    lax.fori_loop(0, count // unroll, step, 0)


def exchange(src, dst, send_sem, recv_sem, where):
    return pltpu.make_async_remote_copy(
        src_ref=src,
        dst_ref=dst,
        send_sem=send_sem,
        recv_sem=recv_sem,
        device_id=where,
        device_id_type=MESH,
    )


def two_terms(x):
    high = x.astype(BF16)
    low = (x - high.astype(F32)).astype(BF16)
    return jnp.concatenate([high, low], axis=0)


def rows_by_region(hot_turned, x):
    return jnp.dot(hot_turned, two_terms(x), preferred_element_type=F32)


def knowledge_rounds(n_gx, n_gy):
    return [
        (along, 2**step)
        for along, size in ((1, n_gy), (0, n_gx))
        for step in range((size - 1).bit_length())
    ]


def kernel(
    n_gx,
    n_gy,
    rows_hbm,
    cols_hbm,
    density_hbm,
    weight_hbm,
    owner_hbm,
    region_hbm,
    face_x_hbm,
    face_y_hbm,
    disp_hbm,
    adj_hbm,
    tiles_hbm,
    filtered_ref,
    compliance_ref,
    rows_ref,
    cols_ref,
    density_ref,
    weight_ref,
    owner_ref,
    region_ref,
    face_x_ref,
    face_y_ref,
    disp_raw,
    adj_raw,
    tiles_raw,
    disp_wide,
    adj_wide,
    tiles_wide,
    turned,
    local,
    ext,
    staged,
    prod,
    prod_swapped,
    onehot,
    hot_turned,
    weights,
    partial,
    totals_out,
    totals_in,
    sums_out,
    sums_in,
    comp_out,
    comp_in,
    load_sem,
    halo_send,
    halo_recv,
    totals_send,
    totals_recv,
    sums_send,
    sums_recv,
    comp_send,
    comp_recv,
    scalar_sem,
    known,
):
    rounds = knowledge_rounds(n_gx, n_gy)
    count = tiles_hbm.shape[0]
    blocks = disp_hbm.shape[0]
    nix = face_x_ref.shape[2]
    niy = face_y_ref.shape[2]
    gx = lax.axis_index("gx")
    gy = lax.axis_index("gy")

    barrier = pltpu.get_barrier_semaphore()

    def each_way(distance, body):
        for side, (place, size, where) in enumerate(
            ((gx, n_gx, lambda d: (gx + d, gy)), (gy, n_gy, lambda d: (gx, gy + d)))
        ):
            if distance < size:

                @pl.when(place + distance < size)
                def _(side=side, where=where):
                    body(side, 0, where(distance))

                @pl.when(place >= distance)
                def _(side=side, where=where):
                    body(side, 1, where(-distance))

    def greet(side, way, where):
        pl.semaphore_signal(barrier, inc=1, device_id=where, device_id_type=MESH)

    each_way(1, greet)

    loads = [
        pltpu.make_async_copy(src, dst, load_sem.at[k])
        for k, (src, dst) in enumerate(
            ((disp_hbm, disp_raw), (adj_hbm, adj_raw), (tiles_hbm, tiles_raw))
        )
    ]
    scalar_loads = [
        pltpu.make_async_copy(src, dst, scalar_sem.at[k])
        for k, (src, dst) in enumerate(
            (
                (face_x_hbm, face_x_ref),
                (face_y_hbm, face_y_ref),
                (rows_hbm, rows_ref),
                (cols_hbm, cols_ref),
                (density_hbm, density_ref),
                (weight_hbm, weight_ref),
                (owner_hbm, owner_ref),
                (region_hbm, region_ref),
            )
        )
    ]
    for load in loads[:2] + scalar_loads + loads[2:]:
        load.start()

    def learn(step, act):
        along, distance = rounds[step]

        def body(side, way, where):
            if side == along:
                act(step, way, where)

        each_way(distance, body)

    def tell(step, way, where):
        pl.semaphore_signal(known.at[step, way], inc=1, device_id=where, device_id_type=MESH)

    def hear(step, way, where):
        pl.semaphore_wait(known.at[step, 1 - way], 1)

    def next_round(step):
        if step > 0:
            learn(step - 1, hear)
        if step < len(rounds):
            learn(step, tell)

    def widen(raw, wide, height):
        def read(c):
            at = pl.ds(pl.multiple_of(c * LANES, LANES), LANES)
            return raw[:, at].astype(F32)

        def write(c, chunk):
            wide[pl.ds(c * (height + 1), height), :] = chunk

        loop(HALF, 4, read, write)

    low_lanes = lax.broadcasted_iota(jnp.int32, (HALF, LANES), 1) < R

    loads[0].wait()
    widen(disp_raw, disp_wide, blocks)
    loads[1].wait()
    widen(adj_raw, adj_wide, blocks)

    def parts(b):
        u = disp_wide[pl.ds(b, HALF, stride=blocks + 1), :]
        a = adj_wide[pl.ds(b, HALF, stride=blocks + 1), :]
        u_turned = pltpu.roll(u, R, 1)
        a_turned = pltpu.roll(a, R, 1)
        even = jnp.where(low_lanes, a, u_turned)
        odd = jnp.where(low_lanes, a_turned, u)
        even_swapped = jnp.where(low_lanes, u, a_turned)
        odd_swapped = jnp.where(low_lanes, u_turned, a)
        block = jnp.concatenate([even, odd], axis=0).astype(BF16)
        swapped = jnp.concatenate([even_swapped, odd_swapped], axis=0).astype(BF16)
        return block, swapped

    def keep_local(b, pair):
        block, swapped = pair
        local[b, :, 0:LANES] = block
        local[b, :, LANES : 2 * LANES] = swapped
        ext[b] = block

    def stage(faces, way, at, number):
        def write(k, block):
            staged[at + k] = block

        loop(number, 4, lambda k: parts(faces[0, way, k])[0], write)

    first = blocks
    plans = (
        (0, first, nix, gx < n_gx - 1, (gx + 1, gy), gx > 0),
        (nix, first + nix, nix, gx > 0, (gx - 1, gy), gx < n_gx - 1),
        (2 * nix, first + 2 * nix, niy, gy < n_gy - 1, (gx, gy + 1), gy > 0),
        (2 * nix + niy, first + 2 * nix + niy, niy, gy > 0, (gx, gy - 1), gy < n_gy - 1),
    )

    def halo(k):
        at, to, number, _, where, _ = plans[k]
        return exchange(
            staged.at[pl.ds(at, number)],
            ext.at[pl.ds(to, number)],
            halo_send.at[k],
            halo_recv.at[k],
            where,
        )

    for load in scalar_loads[:2]:
        load.wait()
    neighbours = (
        (gx > 0).astype(jnp.int32)
        + (gx < n_gx - 1).astype(jnp.int32)
        + (gy > 0).astype(jnp.int32)
        + (gy < n_gy - 1).astype(jnp.int32)
    )
    for k in (1, 0, 3, 2):
        at, to, number, has_target, _, has_source = plans[k]

        @pl.when(has_target)
        def _(k=k, at=at, number=number):
            stage(face_x_ref if k < 2 else face_y_ref, k % 2, at, number)

        if k == 1:
            pl.semaphore_wait(barrier, neighbours)

        @pl.when(has_target)
        def _(k=k):
            halo(k).start()

        @pl.when(jnp.logical_not(has_source))
        def _(to=to, number=number):
            ext[pl.ds(to, number)] = jnp.zeros((number, BS, LANES), BF16)

    next_round(0)
    loop(blocks, 4, parts, keep_local)
    next_round(1)
    for load in scalar_loads[2:]:
        load.wait()

    regions = n_gy * NREG
    key_lane = lax.broadcasted_iota(jnp.int32, (1, regions), 1)

    def key_row(t):
        key = owner_ref[t] * NREG + region_ref[t]
        return (key_lane == key).astype(F32), jnp.full((1, LANES), weight_ref[t], F32)

    def keep_key(t, rows):
        onehot[pl.ds(t, 1), :] = rows[0]
        weights[pl.ds(t, 1), :] = rows[1]

    loop(count, 8, key_row, keep_key)
    hot = onehot[...].astype(BF16)
    hot_turned[...] = jnp.concatenate([hot, hot], axis=0).T
    totals_out[...] = rows_by_region(hot_turned[...], weights[...]).reshape(n_gy, NREG, LANES)
    totals_in[gy] = totals_out[gy]
    next_round(2)

    def totals_copy(j, slot):
        return exchange(
            totals_out.at[j], totals_in.at[slot], totals_send.at[j], totals_recv.at[slot], (gx, j)
        )

    def sums_copy(j, slot):
        return exchange(
            sums_out.at[j], sums_in.at[slot], sums_send.at[j], sums_recv.at[slot], (gx, j)
        )

    me = gx * n_gy + gy

    def comp_copy(d, slot):
        return exchange(
            comp_out,
            comp_in.at[slot],
            comp_send,
            comp_recv,
            (lax.div(d, n_gy), lax.rem(d, n_gy)),
        )

    def all_rows(sem):
        rows = comp_in.at[pl.ds(0, n_gx * n_gy - 1)]
        return pltpu.make_async_copy(rows, rows, sem)

    def others(size, own, body):
        @pl.loop(1, size)
        def _(offset):
            body(lax.rem(own + offset, size))

    loads[2].wait()
    widen(tiles_raw, tiles_wide, count)

    def turn(i):
        t = 2 * i
        one = tiles_wide[pl.ds(t, HALF, stride=count + 1), :]
        two = tiles_wide[pl.ds(t + 1, HALF, stride=count + 1), :]
        even = jnp.where(low_lanes, one, pltpu.roll(two, BS, 1))
        odd = jnp.where(low_lanes, pltpu.roll(one, BS, 1), two)
        return jnp.concatenate([even, odd], axis=0).astype(BF16).T

    def keep_turned(i, value):
        turned[i] = value

    loop(count // 2, 4, turn, keep_turned)
    next_round(3)

    def product(t, i, k):
        return jnp.dot(
            turned[i, k * BS : (k + 1) * BS, :], local[rows_ref[t]], preferred_element_type=F32
        )

    def keep_product(t, result):
        at = pl.ds(pl.multiple_of(t * BS, BS), BS)
        prod[at, :] = result[:, 0:LANES]
        prod_swapped[at, :] = result[:, LANES : 2 * LANES]

    def product_pair(i):
        return product(2 * i, i, 0), product(2 * i + 1, i, 1)

    def keep_pair(i, results):
        keep_product(2 * i, results[0])
        keep_product(2 * i + 1, results[1])

    loop(count // 2, 4, product_pair, keep_pair)
    for step in range(4, len(rounds)):
        next_round(step)
    others(n_gy, gy, lambda j: totals_copy(j, gy).start())

    for k, (_, _, _, _, _, has_source) in enumerate(plans):

        @pl.when(has_source)
        def _(k=k):
            halo(k).wait_recv()

    low8 = lax.broadcasted_iota(jnp.int32, (8, LANES), 1) < R

    def fold(x):
        parts = [x[8 * k : 8 * k + 8, :] for k in range(HALF // 8)]
        return (parts[0] + parts[1]) + (parts[2] + parts[3])

    def element(t):
        base = t * BS
        block = ext[cols_ref[t]]
        even = block[0:HALF, :].astype(F32)
        odd = block[HALF:BS, :].astype(F32)
        at_even = pl.ds(base, HALF, stride=2)
        at_odd = pl.ds(base + 1, HALF, stride=2)
        straight = fold(prod[at_even, :] * even + prod[at_odd, :] * odd)
        crossed = fold(prod_swapped[at_even, :] * even + prod_swapped[at_odd, :] * odd)
        cross = crossed + pltpu.roll(crossed, R, 1)
        strain = straight * (1.0 / math.sqrt(BS))
        rho = density_ref[t]
        sens = cross * (rho * rho * (-3.0 / (2.0 * math.sqrt(BS))))
        return weight_ref[t] * jnp.where(low8, sens, strain), strain

    unroll = 8

    def elements(i, total_energy):
        values = [element(i * unroll + k) for k in range(unroll)]
        for k, (value, strain) in enumerate(values):
            partial[pl.ds((i * unroll + k) * 9, 8), :] = value
            total_energy = total_energy + strain
        return total_energy

    comp = lax.fori_loop(0, count // unroll, elements, jnp.zeros((8, LANES), F32))

    next_round(len(rounds))
    comp_out[...] = jnp.sum(comp, axis=0, keepdims=True)
    comp_in[me] = comp_out[...]
    others(n_gx * n_gy, me, lambda d: comp_copy(d, me).start())

    payload = partial[pl.ds(0, count, stride=9), :]
    for s in range(1, 8):
        payload = payload + partial[pl.ds(s, count, stride=9), :]
    sums_out[...] = rows_by_region(hot_turned[...], payload).reshape(n_gy, NREG, LANES)
    sums_in[gy] = sums_out[gy]
    others(n_gy, gy, lambda j: sums_copy(j, gy).start())

    for k, (_, _, _, has_target, _, _) in enumerate(plans):

        @pl.when(has_target)
        def _(k=k):
            halo(k).wait_send()

    others(n_gy, gy, lambda j: totals_copy(j, gy).wait_send())
    others(n_gy, gy, lambda j: totals_copy(j, j).wait_recv())
    total = jnp.zeros((NREG, LANES), F32)
    for j in range(n_gy):
        total = total + totals_in[j]
    scale = 1.0 / jnp.maximum(total, 1.0)
    all_rows(comp_send).wait()

    others(n_gy, gy, lambda j: sums_copy(j, gy).wait_send())
    others(n_gy, gy, lambda j: sums_copy(j, j).wait_recv())
    gathered = sums_in[0]
    for j in range(1, n_gy):
        gathered = gathered + sums_in[j]
    filtered_ref[...] = gathered * scale

    all_rows(comp_recv).wait()
    unroll = n_gy

    def gather(i, acc):
        for k in range(unroll):
            acc = acc + comp_in[i * unroll + k]
        return acc

    line = lax.fori_loop(0, n_gx, gather, jnp.zeros((1, LANES), F32))
    line = line * (1.0 / math.sqrt(count * n_gx * n_gy))
    turned_line = pltpu.roll(jnp.broadcast_to(line, (8, LANES)), R, 1)
    compliance_ref[...] = turned_line[0, 0:R]


def shards(n_gx, n_gy, *args):
    (
        disp,
        adjoint,
        tiles,
        tile_rows,
        tile_cols,
        density,
        filter_weight,
        owner,
        region,
        face_x,
        face_y,
    ) = args
    count = tiles.shape[0]
    blocks = disp.shape[0]
    faces = face_x.shape[2] * 2 + face_y.shape[2] * 2
    hbm = pl.BlockSpec(memory_space=pltpu.HBM)
    vmem = pl.BlockSpec(memory_space=pltpu.VMEM)
    dma = pltpu.SemaphoreType.DMA
    filtered, compliance = pl.pallas_call(
        functools.partial(kernel, n_gx, n_gy),
        out_shape=(
            jax.ShapeDtypeStruct((NREG, LANES), F32),
            jax.ShapeDtypeStruct((R,), F32),
        ),
        in_specs=[hbm] * 11,
        out_specs=(vmem, vmem),
        scratch_shapes=[
            *(pltpu.SMEM((count,), kind) for kind in (I32, I32, F32, F32, I32, I32)),
            pltpu.SMEM(face_x.shape, I32),
            pltpu.SMEM(face_y.shape, I32),
            pltpu.VMEM((blocks, BS * R), BF16),
            pltpu.VMEM((blocks, BS * R), BF16),
            pltpu.VMEM((count, BS * BS), BF16),
            pltpu.VMEM((HALF * (blocks + 1), LANES), F32),
            pltpu.VMEM((HALF * (blocks + 1), LANES), F32),
            pltpu.VMEM((HALF * (count + 1), LANES), F32),
            pltpu.VMEM((count // 2, 2 * BS, BS), BF16),
            pltpu.VMEM((blocks, BS, 2 * LANES), BF16),
            pltpu.VMEM((blocks + faces, BS, LANES), BF16),
            pltpu.VMEM((faces, BS, LANES), BF16),
            pltpu.VMEM((count * BS, LANES), F32),
            pltpu.VMEM((count * BS, LANES), F32),
            pltpu.VMEM((count, n_gy * NREG), F32),
            pltpu.VMEM((n_gy * NREG, 2 * count), BF16),
            pltpu.VMEM((count, LANES), F32),
            pltpu.VMEM((count * 9, LANES), F32),
            *[pltpu.VMEM((n_gy, NREG, LANES), F32)] * 4,
            pltpu.VMEM((1, LANES), F32),
            pltpu.VMEM((n_gx * n_gy, 1, LANES), F32),
            dma((3,)),
            dma((4,)),
            dma((4,)),
            dma((n_gy,)),
            dma((n_gy,)),
            dma((n_gy,)),
            dma((n_gy,)),
            dma,
            dma,
            dma((8,)),
            pltpu.SemaphoreType.REGULAR((len(knowledge_rounds(n_gx, n_gy)), 2)),
        ],
        compiler_params=pltpu.CompilerParams(
            collective_id=0, has_side_effects=True, vmem_limit_bytes=40 * 2**20
        ),
        name="sensitivities",
    )(*[pltpu.with_memory_space_constraint(x, pltpu.HBM) for x in (
        tile_rows,
        tile_cols,
        density,
        filter_weight,
        owner.reshape(-1),
        region,
        face_x,
        face_y,
        disp,
        adjoint,
        tiles,
    )])
    return filtered, compliance


def solution(mesh):
    placed = (
        P(("gx", "gy"), None),
        P(("gx", "gy"), None),
        P(("gx", "gy"), None),
        P(("gx", "gy")),
        P(("gx", "gy")),
        P(("gx", "gy")),
        P(("gx", "gy")),
        P(("gx", "gy"), None),
        P(("gx", "gy")),
        P(("gx", "gy"), None, None),
        P(("gx", "gy"), None, None),
    )
    return jax.shard_map(
        functools.partial(shards, mesh.shape["gx"], mesh.shape["gy"]),
        mesh=mesh,
        in_specs=placed,
        out_specs=(P(("gx", "gy"), None), P()),
        check_vma=False,
    )
```
